32 devices in a mesh: section: 2 (over x), batch: 16 (over z, y, core).
Axes of the slice: x: 2, y: 2, z: 4, core: 2. Of those that a mesh axis runs over, the one named last changes fastest.
Arguments:
- tokens: bfloat16 [256, 357, 256], P('batch'), may hold values from -6 to 6
- cotangent: bfloat16 [256, 357, 256], P('batch'), may hold values from -6 to 6
- frame_ids: int32 [256, 357], P('batch'), may hold values from 0 to 21, as said below
- attend_gain: float32 [2, 256], P('section'), may hold values from 0.1 to 1.9
- attend_shift: float32 [2, 256], P('section'), may hold values from -4 to 4
- inward_weight: bfloat16 [2, 256, 768], P('section'), may hold values from -0.375 to 0.375
- inward_bias: float32 [2, 512], P('section'), may hold values from -4 to 4
- outward_weight: bfloat16 [2, 256, 256], P('section'), may hold values from -1.5 to 1.5
- outward_bias: float32 [2, 256], P('section'), may hold values from -4 to 4
- mixing_gain: float32 [2, 256], P('section'), may hold values from 0.1 to 1.9
- mixing_shift: float32 [2, 256], P('section'), may hold values from -4 to 4
- up_weight: bfloat16 [2, 256, 1024], P('section'), may hold values from -0.375 to 0.375
- up_bias: float32 [2, 1024], P('section'), may hold values from -4 to 4
- down_weight: bfloat16 [2, 1024, 256], P('section'), may hold values from -0.1875 to 0.1875
- down_bias: float32 [2, 256], P('section'), may hold values from -4 to 4
Outputs:
- layer_out: bfloat16 [256, 357, 256], P('batch', None, 'section')
- input_grad: float32 [256, 357, 256], P('batch', None, 'section')
- attend_gain_grad: float32 [2, 256], P('section')
- attend_shift_grad: float32 [2, 256], P('section')
- inward_weight_grad: float32 [2, 256, 768], P('section')
- inward_bias_grad: float32 [2, 512], P('section')
- outward_weight_grad: float32 [2, 256, 256], P('section')
- outward_bias_grad: float32 [2, 256], P('section')
- mixing_gain_grad: float32 [2, 256], P('section')
- mixing_shift_grad: float32 [2, 256], P('section')
- up_weight_grad: float32 [2, 256, 1024], P('section')
- up_bias_grad: float32 [2, 1024], P('section')
- down_weight_grad: float32 [2, 1024, 256], P('section')
- down_bias_grad: float32 [2, 256], P('section')
The draws below stay inside these ranges and needn't reach their ends.
Inputs may be any that keep to these rules, and one draw needn't show every extreme that they name: `frame_ids`: in each sequence the frame ids start at 0 and rise by one every 17 tokens; the first frame holds 1 to 17 tokens, every later frame 17 tokens except that the last may be cut short.
All inputs are finite; a program needn't handle non-finite values.
Results may differ from the reference program's by a relative error of at most 0.014.
Values may be sent and summed in bfloat16 or wider, within the bound.
No kernel may reach another device: no remote copies, remote signals or barrier semaphores. Data moves between devices by JAX's collectives and lax.ppermute only.
A program may use at most 320 MiB of HBM per device.

```python
import math
import jax
import jax.numpy as jnp
from jax import lax

D = 256
HEADS = 4
HEAD_DIM = 64
FF = 1024
SEQ = 357
FRAME_TOKENS = 17
SEQS = 256
N_SECTION = 2


def draw_frame_ids(key, part):
    key = jax.random.fold_in(key, 5)
    starts = jax.random.randint(key, (SEQS,), 0, FRAME_TOKENS)
    starts = starts.at[0].set(FRAME_TOKENS - 1)
    places = jnp.arange(SEQ, dtype=jnp.int32)
    return ((places[None, :] + starts[:, None]) // FRAME_TOKENS).astype(jnp.int32)


def shard_levels(rng, extent, split, smallest, largest):
    factor_of = 1.0
    for dim, blocks in split:
        steps = jax.random.uniform(jax.random.fold_in(jax.random.fold_in(rng, 6), dim), (blocks,), jnp.float32, smallest / len(split), largest / len(split))
        factor_of = factor_of * jnp.repeat(jnp.exp(steps), extent[dim] // blocks).reshape((-1,) + (1,) * (len(extent) - 1 - dim))
    return factor_of


def bell_draw(own_key, extent, scale, bound, pieces=(), kind=jnp.bfloat16):
    values = scale * jax.random.normal(own_key, extent, jnp.float32)
    if pieces:
        values = values * shard_levels(own_key, extent, pieces, -0.22, 0.18)
    return jnp.clip(values, -bound, bound).astype(kind)


def setup_inputs(seed: int = 0) -> dict:
    streams_of = jax.random.split(jax.random.key(seed), 16)
    return {
        "tokens": bell_draw(streams_of[0], (SEQS, SEQ, D), 1.0, 6.0, ((0, 16),)),
        "cotangent": bell_draw(streams_of[1], (SEQS, SEQ, D), 1.0, 6.0, ((0, 16),)),
        "frame_ids": draw_frame_ids(jax.random.fold_in(streams_of[15], 71), 0),
        "attend_gain": jnp.clip(1.0 + 0.18 * jax.random.normal(streams_of[3], (N_SECTION, D), jnp.float32), 0.1, 1.9),
        "attend_shift": bell_draw(streams_of[4], (N_SECTION, D), 0.3, 4.0, ((0, 2),), jnp.float32),
        "inward_weight": bell_draw(streams_of[5], (N_SECTION, D, 3 * D), D ** -0.5, 0.375, ((0, 2),)),
        "inward_bias": bell_draw(streams_of[6], (N_SECTION, 2 * D), 0.3, 4.0, ((0, 2),), jnp.float32),
        "outward_weight": bell_draw(streams_of[7], (N_SECTION, D, D), (D // 16) ** -0.5, 1.5, ((0, 2),)),
        "outward_bias": bell_draw(streams_of[8], (N_SECTION, D), 0.3, 4.0, ((0, 2),), jnp.float32),
        "mixing_gain": jnp.clip(1.0 + 0.18 * jax.random.normal(streams_of[9], (N_SECTION, D), jnp.float32), 0.1, 1.9),
        "mixing_shift": bell_draw(streams_of[10], (N_SECTION, D), 0.3, 4.0, ((0, 2),), jnp.float32),
        "up_weight": bell_draw(streams_of[11], (N_SECTION, D, FF), D ** -0.5, 0.375, ((0, 2),)),
        "up_bias": bell_draw(streams_of[12], (N_SECTION, FF), 0.3, 4.0, ((0, 2),), jnp.float32),
        "down_weight": bell_draw(streams_of[13], (N_SECTION, FF, D), FF ** -0.5, 0.1875, ((0, 2),)),
        "down_bias": bell_draw(streams_of[14], (N_SECTION, D), 0.3, 4.0, ((0, 2),), jnp.float32),
    }


@jax.custom_vjp
def low(v):
    return lax.optimization_barrier(v.astype(jnp.bfloat16)).astype(jnp.float32)

@jax.custom_vjp
def low_back(v):
    return v

def low_keep(v):
    return (low(v), None)

def low_pass(kept, grad):
    return (grad,)

def back_keep(v):
    return (v, None)

def back_low(kept, grad):
    return (low(grad),)
low.defvjp(low_keep, low_pass)
low_back.defvjp(back_keep, back_low)
epsilon = 1e-05
masked_value = -1e+30
highest = lax.Precision.HIGHEST

def normalize(value, gain, shift):
    center = value - lax.optimization_barrier(jnp.mean(value, axis=-1, keepdims=True))
    spread = lax.optimization_barrier(jnp.mean(center * center, axis=-1, keepdims=True))
    return center * lax.rsqrt(spread + epsilon) * gain + shift

def matmul(left, right):
    return jnp.dot(left, right, precision=highest)

def layer(inputs, frames, weights):
    attend_gain, attend_shift, inward_weight, inward_bias, outward_weight, outward_bias, mixing_gain, mixing_shift, up_weight, up_bias, down_weight, down_bias = weights
    sequences, length = frames.shape
    normed = low(normalize(inputs, attend_gain, attend_shift))
    bias_full = jnp.concatenate([inward_bias[:D], jnp.zeros((D,), jnp.float32), inward_bias[D:]])
    packed = low_back(low(matmul(normed, inward_weight) + bias_full))
    packed = packed.reshape(sequences, length, 3, HEADS, HEAD_DIM)
    queries, keys, values = (packed[:, :, 0], packed[:, :, 1], packed[:, :, 2])
    scores = jnp.einsum('bqhd,bkhd->bhqk', queries, keys, precision=highest) * HEAD_DIM ** (-0.5)
    scores = low_back(scores)
    allowed = frames[:, None, None, :] <= frames[:, None, :, None]
    scores = jnp.where(allowed, scores, masked_value)
    probs = low(jax.nn.softmax(scores, axis=-1))
    mixed = jnp.einsum('bhqk,bkhd->bqhd', probs, values, precision=highest)
    mixed = low_back(low(mixed)).reshape(sequences * length, D)
    middle = inputs + low_back(matmul(mixed, outward_weight) + outward_bias)
    second = low(normalize(middle, mixing_gain, mixing_shift))
    raised = low_back(matmul(second, up_weight) + up_bias)
    activated = low(jax.nn.gelu(raised, approximate=False))
    return middle + low_back(matmul(activated, down_weight) + down_bias)

def network(inputs, params, frames):
    first = tuple((item[0] for item in params))
    second = tuple((item[1] for item in params))
    between = low_back(low(layer(inputs, frames, first)))
    return layer(between, frames, second)

def reference(tokens, cotangent, frame_ids, attend_gain, attend_shift, inward_weight, inward_bias, outward_weight, outward_bias, mixing_gain, mixing_shift, up_weight, up_bias, down_weight, down_bias):
    params = tuple((item.astype(jnp.float32) for item in (attend_gain, attend_shift, inward_weight, inward_bias, outward_weight, outward_bias, mixing_gain, mixing_shift, up_weight, up_bias, down_weight, down_bias)))
    group = math.gcd(SEQS, 8)
    count = SEQS // group

    def advance(totals, item):
        inputs, tangent, frames = item
        flat = inputs.astype(jnp.float32).reshape(group * SEQ, D)
        result, backward = jax.vjp(lambda first, second: network(first, second, frames), flat, params)
        grad_input, grad_params = backward(tangent.astype(jnp.float32).reshape(group * SEQ, D))
        totals = jax.tree.map(lambda left, right: left + right, totals, grad_params)
        return (totals, (result.astype(jnp.bfloat16).reshape(group, SEQ, D), grad_input.reshape(group, SEQ, D)))
    zeros = jax.tree.map(jnp.zeros_like, params)
    totals, (outputs, gradients) = lax.scan(advance, zeros, (tokens.reshape(count, group, SEQ, D), cotangent.reshape(count, group, SEQ, D), frame_ids.reshape(count, group, SEQ)))
    return (outputs.reshape(SEQS, SEQ, D), gradients.reshape(SEQS, SEQ, D), totals[0], totals[1], totals[2], totals[3], totals[4], totals[5], totals[6], totals[7], totals[8], totals[9], totals[10], totals[11])
```

```python
import functools
from types import SimpleNamespace

import jax
import jax.numpy as jnp
from jax import lax
from jax.experimental import pallas as pl
from jax.experimental.layout import Layout, with_layout_constraint
from jax.experimental.pallas import tpu as pltpu
from jax.sharding import PartitionSpec as P

HEADS = 4
WHOLE_FRAME = 17

epsilon = 1e-05
masked_value = -1e30
log2e = 1.4426950408889634

PAIR = 2
LIVE = 368
ROWS = 384
BOTH = PAIR * ROWS
USED = BOTH - ROWS + LIVE
ONES = 16
STEP = 48
CHUNKS = tuple((at, min(STEP, LIVE - at)) for at in range(0, LIVE, STEP))
MEMBERS = tuple(range(PAIR))
TILES = ((0, 144, 0), (128, 272, 128), (256, 368, 256))
STACK = (0, 144, 416)
STACKED = 784

bf16 = jnp.bfloat16
f32 = jnp.float32


def dot(left, right):
    return jnp.dot(left, right, preferred_element_type=f32)


def dot_upper(left, right):
    return lax.dot_general(left, right, (((1,), (1,)), ((), ())), preferred_element_type=f32)


def gelu_pair(value):
    half = 0.5 + 0.5 * lax.erf(value * 0.7071067811865476)
    bell = jnp.exp2(value * value * (-0.5 * log2e) - 1.3257480647361595)
    return value * half, half + value * bell


def tree(op, parts):
    parts = list(parts)
    while len(parts) > 1:
        pairs = [op(a, b) for a, b in zip(parts[0::2], parts[1::2])]
        parts = pairs + parts[len(parts) // 2 * 2 :]
    return parts[0]


def eights(value):
    return [value[at : at + 8] for at in range(0, value.shape[0], 8)]


def twice(stat):
    return jnp.concatenate([stat, stat], axis=1)


def row_mean(value):
    mean = jnp.mean(value, axis=-1, keepdims=True)
    return jnp.broadcast_to(mean, (value.shape[0], 128))


def normalize(load, T, scales, store):
    for _, _, _, rows in chunks():
        T.mean[rows, :] = row_mean(load(rows))
    for _, _, _, rows in chunks():
        center = load(rows) - twice(T.mean[rows, :])
        T.spread[rows, :] = row_mean(center * center)
    for _, _, _, rows in chunks():
        scale = lax.rsqrt(T.spread[rows, :] + epsilon)
        scales[rows, :] = scale.astype(bf16)
        store(rows, (load(rows) - twice(T.mean[rows, :])) * twice(scale))


def norm_back(gain, g, normed, scales, T, store):
    for _, _, _, rows in chunks():
        gn = g[rows, :] * gain
        T.mean[rows, :] = row_mean(gn)
        T.slope[rows, :] = row_mean(gn * normed[rows, :].astype(f32))
    for chunk in chunks():
        rows = chunk[3]
        gn = g[rows, :] * gain - twice(T.mean[rows, :])
        back = gn - normed[rows, :].astype(f32) * twice(T.slope[rows, :])
        store(chunk, twice(scales[rows, :].astype(f32)) * back)


def masked_pair(value, head):
    lane = lax.broadcasted_iota(jnp.int32, value.shape, 1)
    keep = (lane < 64) if head % 2 == 0 else (lane >= 64)
    return jnp.where(keep, value, jnp.zeros_like(value))


def pair_lanes(head):
    return slice(128 * (head // 2), 128 * (head // 2) + 128)


def two_heads(ref, p, rows):
    value = ref[rows, 128 * p : 128 * p + 128]
    return jnp.concatenate([masked_pair(value, 0), masked_pair(value, 1)], axis=0)


def column_of(t, side):
    return slice(256 * t + 128 * side, 256 * t + 128 * side + 128)


def stack_of(t):
    return slice(STACK[t], STACK[t] + TILES[t][1])


def of(member, start, stop):
    return slice(member * ROWS + start, member * ROWS + stop)


def chunks():
    for member in MEMBERS:
        for at, size in CHUNKS:
            yield member, at, size, pl.ds(member * ROWS + at, size)


def clear_tails(*refs):
    for ref in refs:
        for member in MEMBERS:
            rows = of(member, LIVE, ROWS)
            ref[rows, :] = jnp.zeros((ROWS - LIVE,) + ref.shape[1:], ref.dtype)


def forward_attend(x, lines, W, S, T):
    vec = W.vec

    def first(rows, n):
        S.n1[rows, :] = n.astype(bf16)
        T.a[rows, :] = (n * vec[:, 0:256] + vec[:, 256:512]).astype(bf16)

    normalize(lambda rows: x[rows, :].astype(f32), T, S.r1, first)
    clear_tails(S.n1)
    a = T.a[0:USED, :]
    packed = dot(a, W.inw[...])
    T.k[0:USED, :] = packed[:, 256:512].astype(bf16)
    S.q[0:USED, :] = (packed[:, 0:256] + vec[:, 512:768]).astype(bf16)
    S.v[0:USED, :] = (packed[:, 512:768] + vec[:, 768:1024]).astype(bf16)
    clear_tails(T.k, S.q, S.v)
    for member in MEMBERS:
        frames = lines[member]
        length = frames.shape[1]
        first = jnp.sum((frames == 0).astype(f32), axis=1, keepdims=True).astype(jnp.int32)
        last = jnp.minimum(first - 1 + WHOLE_FRAME * frames, length - 1)
        T.last[:, :] = jnp.full((1, ROWS), length - 1, jnp.int32)
        T.last[:, 0:length] = last
        for t, (at, stop, sure) in enumerate(TILES):
            keys = lax.broadcasted_iota(jnp.int32, (stop - sure, 128), 0) + sure
            seen = keys <= T.last[:, at : at + 128]
            T.mask[member, t, 0 : stop - sure, :] = jnp.where(seen, 0.0, masked_value)
    power = 0.125 * log2e
    units = [(p, member) for p in range(2) for member in MEMBERS]

    def scores(u):
        p, member = units[u]
        for t, (at, stop, _) in enumerate(TILES):
            T.s[u % 3, 0:stop, 256 * t : 256 * t + 256] = dot_upper(
                T.k[of(member, 0, stop), 128 * p : 128 * p + 128],
                two_heads(S.q, p, of(member, at, at + 128)),
            )

    def strips(u, t, side):
        _, stop, sure = TILES[t]
        for start in range(0, stop, 16):
            value = T.s[u % 3, start : start + 16, column_of(t, side)]
            if start >= sure:
                value = value + T.mask[units[u][1], t, start - sure : start - sure + 16, :]
            yield start, value

    columns = [(t, side) for t in range(3) for side in range(2)]

    def peaks(u):
        for t, side in columns:
            tops = [tree(jnp.maximum, eights(value)) for _, value in strips(u, t, side)]
            peak = jnp.max(tree(jnp.maximum, tops), axis=0, keepdims=True)
            T.peak[u % 3, :, column_of(t, side)] = peak * power

    def raises(u):
        for t, side in columns:
            lanes = column_of(t, side)
            peak = T.peak[u % 3, :, lanes]
            sums = []
            for start, value in strips(u, t, side):
                value = jnp.exp2(value * power - peak)
                T.s[u % 3, start : start + 16, lanes] = value
                sums.append(value[0:8] + value[8:16])
            total = jnp.sum(tree(jnp.add, sums), axis=0, keepdims=True)
            T.share[u % 3, :, lanes] = 1.0 / total

    def shares(u):
        p, member = units[u]
        for t, side in columns:
            lanes = column_of(t, side)
            share = T.share[u % 3, :, lanes]
            for start in range(0, TILES[t][1], 16):
                value = T.s[u % 3, start : start + 16, lanes] * share
                rows = slice(STACK[t] + start, STACK[t] + start + 16)
                S.pT[member, p, rows, 128 * side : 128 * side + 128] = value.astype(bf16)

    def mix(u):
        p, member = units[u]
        for t, (at, stop, _) in enumerate(TILES):
            both = dot(
                T.vT[128 * p : 128 * p + 128, of(member, 0, stop)],
                S.pT[member, p, stack_of(t), :],
            )
            for side in range(2):
                feats = slice(128 * p + 64 * side, 128 * p + 64 * side + 64)
                value = both[64 * side : 64 * side + 64, 128 * side : 128 * side + 128]
                S.mT[feats, of(member, at, at + 128)] = value.astype(bf16)

    scores(0)
    T.vT[...] = S.v[...].T
    peaks(0)
    scores(1)
    S.kT[...] = T.k[...].T
    raises(0)
    peaks(1)
    for u in range(len(units)):
        if u + 2 < len(units):
            scores(u + 2)
        shares(u)
        if u + 1 < len(units):
            raises(u + 1)
        if u + 2 < len(units):
            peaks(u + 2)
        mix(u)
    S.mT[256 : 256 + ONES, :] = jnp.ones((ONES, BOTH), bf16)
    mixed = S.mT[0:256, :].T
    T.f[...] = dot(mixed[0:USED], W.outw[...])
    for _, _, _, rows in chunks():
        S.middle[rows, :] = x[rows, :].astype(f32) + (T.f[rows, :] + vec[:, 1024:1280])

    def second(rows, n):
        S.n2[rows, :] = n.astype(bf16)
        S.second[rows, :] = (n * vec[:, 1280:1536] + vec[:, 1536:1792]).astype(bf16)

    normalize(lambda rows: S.middle[rows, :], T, S.r2, second)
    clear_tails(S.n2, S.second)


def forward_feed(W, S, T, out):
    vec = W.vec
    second = S.second[0:USED, :]

    T.g[...] = dot(second, W.upw[...])
    for c in range(4):
        cols = slice(256 * c, 256 * c + 256)
        for member, at, size, rows in chunks():
            bias = vec[:, 1792 + 256 * c : 2048 + 256 * c]
            act, slope = gelu_pair(T.g[rows, cols] + bias)
            S.act[rows, cols] = act.astype(bf16)
            S.dg[rows, cols] = slope.astype(bf16)
    clear_tails(S.act, S.dg)
    T.g[:, 0:256] = dot(S.act[0:USED, :], W.dnw[...])
    for member, at, size, rows in chunks():
        out(member, at, size, S.middle[rows, :] + (T.g[rows, 0:256] + vec[:, 2816:3072]))


def backward_feed(e_ref, W, S, T, acc):
    vec = W.vec
    e = e_ref[0:USED, :]
    eT = e_ref[...].T
    T.n2T[0:256, :] = S.n2[...].T

    T.g[...] = dot_upper(e, W.dnw[...])
    downs = dot(eT, S.act[...])
    for c in range(4):
        cols = slice(256 * c, 256 * c + 256)
        acc[4 + c, 0:256, :] += downs[:, cols]
        for member, at, size, rows in chunks():
            slope = S.dg[rows, cols].astype(f32)
            T.gr[rows, cols] = (T.g[rows, cols] * slope).astype(bf16)
    T.g[:, 0:256] = dot_upper(T.gr[0:USED, :], W.upw[...])
    ups = dot(T.n2T[...], T.gr[...])
    for c in range(4):
        acc[c] += ups[:, 256 * c : 256 * c + 256]
    columns = []

    def middle(chunk, back):
        rows = chunk[3]
        incoming = e_ref[rows, :].astype(f32)
        columns.append(tree(jnp.add, eights(incoming)))
        middle = incoming + back
        T.gmiddle[rows, :] = middle
        T.gp[rows, :] = middle.astype(bf16)

    norm_back(vec[:, 1280:1536], T.g.at[:, 0:256], S.n2, S.r2, T, middle)
    acc[4, 256 : 256 + ONES, :] += jnp.sum(tree(jnp.add, columns), axis=0, keepdims=True)


def backward_attend(W, S, T, acc, out):
    vec = W.vec
    gp = T.gp[...]
    T.gm[0:USED, :] = dot_upper(gp[0:USED], W.outw[...]).astype(bf16)
    T.n1T[0:256, :] = S.n1[...].T
    gmT = dot_upper(W.outw[...], gp)
    for h in range(HEADS):
        feats = slice(64 * h, 64 * h + 64)
        product = gmT[feats] * S.mT[feats, :].astype(f32)
        T.inner[h : h + 1, :] = jnp.sum(product, axis=0, keepdims=True)
    units = [(p, member) for p in range(2) for member in MEMBERS]

    def slopes(u):
        p, member = units[u]
        for t, (at, stop, _) in enumerate(TILES):
            queries = of(member, at, at + 128)
            gprobs = dot_upper(
                S.v[of(member, 0, stop), 128 * p : 128 * p + 128], two_heads(T.gm, p, queries)
            )
            probs = S.pT[member, p, stack_of(t), :].astype(f32)
            inner = [T.inner[2 * p + side : 2 * p + side + 1, queries] for side in range(2)]
            slope = probs * (gprobs - jnp.concatenate(inner, axis=1))
            T.ds[u % 2, stack_of(t), :] = slope.astype(bf16)

    def gather(parts, scale=None):
        start = 0
        for t, (_, stop, _) in enumerate(TILES):
            value = tree(jnp.add, [part[start:stop] for part in parts[t:]])
            value = value if scale is None else value * scale
            yield start, stop, value.astype(bf16)
            start = stop

    def products(u):
        p, member = units[u]
        gk, gv = [], []
        for t, (at, stop, _) in enumerate(TILES):
            queries = of(member, at, at + 128)
            ds = T.ds[u % 2, stack_of(t), :]
            gk.append(dot(ds, two_heads(S.q, p, queries)))
            gv.append(dot(S.pT[member, p, stack_of(t), :], two_heads(T.gm, p, queries)))
            both = dot(S.kT[128 * p : 128 * p + 128, of(member, 0, stop)], ds) * 0.125
            for side in range(2):
                feats = slice(128 * p + 64 * side, 128 * p + 64 * side + 64)
                value = both[64 * side : 64 * side + 64, 128 * side : 128 * side + 128]
                T.gqT[feats, queries] = value.astype(bf16)
        for start, stop, value in gather(gk, 0.125):
            T.gqkv[of(member, start, stop), 256 + 128 * p : 384 + 128 * p] = value
        for start, stop, value in gather(gv):
            T.gqkv[of(member, start, stop), 512 + 128 * p : 640 + 128 * p] = value

    slopes(0)
    acc[3] += dot(S.mT[...], gp)
    for u in range(len(units)):
        if u + 1 < len(units):
            slopes(u + 1)
        products(u)
    T.gqkv[:, 0:256] = T.gqT[...].T
    T.g[:, 0:256] = dot_upper(T.gqkv[0:USED, :], W.inw[...])
    ins = dot(T.n1T[...], T.gqkv[...])
    for b in range(3):
        acc[b] += ins[:, 256 * b : 256 * b + 256]

    def finish(chunk, back):
        member, at, size, rows = chunk
        out(member, at, size, T.gmiddle[rows, :] + back)

    norm_back(vec[:, 0:256], T.g.at[:, 0:256], S.n1, S.r1, T, finish)


ATTEND_SAVED = dict(
    n1=((BOTH, 256), bf16, 0),
    r1=((BOTH, 128), bf16, 0),
    v=((BOTH, 256), bf16, 0),
    kT=((256, BOTH), bf16, 1),
    q=((BOTH, 256), bf16, 0),
    pT=((PAIR, 2, STACKED, 256), bf16, 0),
    mT=((256 + ONES, BOTH), bf16, 1),
    n2=((BOTH, 256), bf16, 0),
    r2=((BOTH, 128), bf16, 0),
)
BETWEEN = dict(second=((BOTH, 256), bf16, 0), middle=((BOTH, 256), f32, 0))
GELU_SAVED = dict(act=((BOTH, 1024), bf16, 0), dg=((BOTH, 1024), bf16, 0))
ATTEND_SCRATCH = dict(
    a=((BOTH, 256), bf16, 0),
    k=((BOTH, 256), bf16, 0),
    vT=((256, BOTH), bf16, 1),
    last=((1, ROWS), jnp.int32, 0),
    mask=((PAIR, 3, 144, 128), f32, 0),
    s=((3, LIVE, 2 * ROWS), f32, 0),
    peak=((3, 1, 2 * ROWS), f32, 0),
    share=((3, 1, 2 * ROWS), f32, 0),
    mean=((BOTH, 128), f32, 0),
    spread=((BOTH, 128), f32, 0),
    f=((USED, 256), f32, 0),
    x=((BOTH, 256), bf16, 0),
)
BACK_SCRATCH = dict(
    mean=((BOTH, 128), f32, 0),
    slope=((BOTH, 128), f32, 0),
    g=((USED, 1024), f32, 0),
    gr=((BOTH, 1024), bf16, 0),
    gp=((BOTH, 256), bf16, 0),
    gmiddle=((BOTH, 256), f32, 0),
    n1T=((256 + ONES, BOTH), bf16, 1),
    n2T=((256 + ONES, BOTH), bf16, 1),
    gm=((BOTH, 256), bf16, 0),
    inner=((8, BOTH), f32, 0),
    ds=((2, STACKED, 256), bf16, 0),
    gqT=((256, BOTH), bf16, 0),
    gqkv=((BOTH, 768), bf16, 0),
)
ATTEND_WEIGHTS = dict(
    vec=((1, 3072), f32, 0),
    inw=((256, 768), bf16, 0),
    outw=((256, 256), bf16, 0),
)
WEIGHTS = dict(
    upw=((256, 1024), bf16, 0),
    dnw=((1024, 256), bf16, 0),
)
FEED_WEIGHTS = dict(WEIGHTS, vec=ATTEND_WEIGHTS["vec"])
WEIGHTS = dict(ATTEND_WEIGHTS, **WEIGHTS)
ACC = dict(
    feed=((8, 256 + ONES, 256), f32, 0),
    attend=((4, 256 + ONES, 256), f32, 0),
)
FEED_HALF = 8 * 256 + 128
ATTEND_HALF = 4 * 256 + 128
WIRE = FEED_HALF + ATTEND_HALF
VMEM_LIMIT = 62 * 1024 * 1024


def load_padded(ref, member, source, length):
    whole = length // 16 * 16
    ref[of(member, whole, ROWS), :] = jnp.zeros((ROWS - whole, 256), bf16)
    ref[of(member, 0, length), :] = source[...]


def fetch_weights(refs, layer, place, attend, feed=None, meanwhile=None):
    vec, inw, outw = attend
    core = place[2]

    def run(pairs):
        copies = [
            pltpu.make_async_copy(source, target, refs.sem.at[i])
            for i, (source, target) in enumerate(pairs)
        ]
        for copy in copies:
            copy.start()
        if meanwhile is not None:
            meanwhile()
        for copy in copies:
            copy.wait()

    @pl.when(place[1] == layer)
    def _():
        pairs = [(refs.own[0], vec)]
        if inw is not None:
            pairs += [(refs.own[1], inw), (refs.own[2], outw)]
        if feed is not None:
            pairs += list(zip(refs.own[3:], feed))
        run(pairs)

    @pl.when(place[1] != layer)
    def _():
        pairs = [(refs.far[0].at[128:144, :], refs.bits)]
        if inw is not None:
            for i in range(2):
                at = (core if i == 0 else 1 - core) * 128
                rows = pl.ds(pl.multiple_of(at, 128), 128)
                pairs.append((refs.far[i].at[0:128, 0:768], inw.at[rows, :]))
                pairs.append((refs.far[i].at[0:128, 768:1024], outw.at[rows, :]))
        if feed is not None:
            upw, dnw = feed
            for i in range(2):
                part = refs.far[2 + i]
                at = core if i == 0 else 1 - core
                rows = pl.ds(pl.multiple_of(at * 128, 128), 128)
                pairs.append((part.at[0:128, :], upw.at[rows, :]))
                for j in range(4):
                    rows = pl.ds(pl.multiple_of(at * 512 + 128 * j, 128), 128)
                    lanes = slice(256 * j, 256 * j + 256)
                    pairs.append((part.at[128:256, lanes], dnw.at[rows, :]))
        run(pairs)
        parts = refs.bits[...].astype(f32)
        for j in range(3):
            value = parts[j : j + 1] + parts[3 + j : 4 + j] + parts[6 + j : 7 + j]
            vec[:, 1024 * j : 1024 * j + 1024] = value


def emit_rows(target, at, blocks):
    tail = at + 512 * len(blocks)
    target[tail : tail + 128, :] = jnp.zeros((128, 128), target.dtype)
    for j, block in enumerate(blocks):
        for side in range(2):
            lanes = slice(128 * side, 128 * side + 128)
            part = 2 * j + side
            target[at + 256 * part : at + 256 * part + 256, :] = block[0:256, lanes].astype(
                target.dtype
            )
            target[tail + ONES * part : tail + ONES * part + ONES, :] = block[
                256 : 256 + ONES, lanes
            ].astype(target.dtype)


def emit_half(target, at, half, acc):
    emit_rows(target, at, [acc.feed.at[4 * half + b] for b in range(4)])
    emit_rows(target, at + FEED_HALF, [acc.attend.at[2 * half + b] for b in range(2)])


def emit_halves(refs, core):
    for half in range(2):

        @pl.when(core == half)
        def _(half=half):
            emit_half(refs.keep, 0, half, refs)
            emit_half(refs.send, 0, 1 - half, refs)


def pack_kernel(place, *refs):
    vec, half = refs[-2:]
    inw, outw = refs[8:10]
    at = 0
    for ref in refs[:8]:
        vec[:, at : at + ref.shape[1]] = ref[...]
        at += ref.shape[1]
    rows = pl.ds(pl.multiple_of(place[2] * 128, 128), 128)
    half[0:128, 0:768] = inw[0, rows, :]
    half[0:128, 768:1024] = outw[0, rows, :]
    rest = jnp.concatenate([vec[:, 1024 * j : 1024 * j + 1024] for j in range(3)], axis=0)
    parts = []
    for _ in range(3):
        part = rest.astype(bf16).astype(f32)
        parts.append(part)
        rest = rest - part
    parts.append(jnp.zeros((7, 1024), f32))
    half[128:144, :] = jnp.concatenate(parts, axis=0).astype(bf16)


def pack_feed_kernel(place, upw, dnw, half):
    half[0:128, :] = upw[0, pl.ds(pl.multiple_of(place[2] * 128, 128), 128), :]
    for j in range(4):
        rows = pl.ds(pl.multiple_of(place[2] * 512 + 128 * j, 128), 128)
        half[128:256, 256 * j : 256 * j + 256] = dnw[0, rows, :]


def zero(refs):
    for ref in refs:
        ref[...] = jnp.zeros(ref.shape, ref.dtype)


def set_ones(*refs):
    for ref in refs:
        ref[256 : 256 + ONES, :] = jnp.ones((ONES, BOTH), bf16)


def attend_kernel(place, refs):
    step = pl.program_id(0)

    @pl.when(step == 0)
    def _():
        fetch_weights(refs, 0, place, (refs.vec, refs.inw, refs.outw))

    length = refs.frames.shape[1]
    lines = []
    for member in MEMBERS:
        load_padded(refs.x, member, refs.tokens.at[member], length)
        lines.append(refs.frames[pl.ds(place[0] + PAIR * step + member, 1), :])
    forward_attend(refs.x, lines, refs, refs, refs)


def middle_kernel(place, refs):
    step = pl.program_id(0)

    @pl.when(step == 0)
    def _():
        def clear():
            zero([refs.feed, refs.attend])
            clear_tails(refs.gqkv, refs.gr, refs.gp, refs.gm, refs.x, refs.low_second)
            set_ones(refs.n1T, refs.n2T)

        held = (refs.low_vec, None, None)
        fetch_weights(refs, 0, place, held, (refs.low_upw, refs.low_dnw), clear)
        held = (refs.vec, refs.inw, refs.outw)
        fetch_weights(refs, 1, place, held, (refs.upw, refs.dnw))

    length = refs.frames.shape[1]
    upper = place[1] > 0
    lower = SimpleNamespace(upw=refs.low_upw, dnw=refs.low_dnw, vec=refs.low_vec)
    below = SimpleNamespace(
        second=refs.low_second, middle=refs.low_middle, act=refs.low_act, dg=refs.low_dg
    )

    def out_lower(member, at, size, rows):
        refs.x[of(member, at, at + size), :] = rows.astype(bf16)

    def out(member, at, size, rows):
        size = min(size, length - at)
        rows = rows[:size].astype(bf16)
        low, high = rows[:, 0:128], rows[:, 128:256]
        refs.mine[member, at : at + size, :] = jnp.where(upper, high, low)
        refs.other[member, at : at + size, :] = jnp.where(upper, low, high)

    def out_back(member, at, size, rows):
        refs.e0[of(member, at, at + size), :] = rows.astype(bf16)

    lines = []
    for member in MEMBERS:
        load_padded(refs.e, member, refs.cotangent.at[member], length)
        lines.append(refs.frames[pl.ds(place[0] + PAIR * step + member, 1), :])
    for member, at, size, rows in chunks():
        n = refs.low_n2[rows, :].astype(f32)
        second = n * refs.low_vec[:, 1280:1536] + refs.low_vec[:, 1536:1792]
        refs.low_second[rows, :] = second.astype(bf16)
    forward_feed(lower, below, refs, out_lower)
    forward_attend(refs.x, lines, refs, refs, refs)
    forward_feed(refs, refs, refs, out)
    backward_feed(refs.e, refs, refs, refs, refs.feed)
    clear_tails(refs.e0)
    backward_attend(refs, refs, refs, refs.attend, out_back)

    @pl.when(step == pl.num_programs(0) - 1)
    def _():
        emit_halves(refs, place[2])


DEFERRED = ("v", "kT", "q", "pT", "mT", "n1", "r1")


def back_kernel(place, refs):
    step = pl.program_id(0)

    @pl.when(step == 0)
    def _():
        def clear():
            zero([refs.feed, refs.attend])
            clear_tails(refs.gqkv, refs.gr, refs.gp, refs.gm)
            set_ones(refs.n1T, refs.n2T)

        held = (refs.vec, refs.inw, refs.outw)
        fetch_weights(refs, 0, place, held, (refs.upw, refs.dnw), clear)

    length = refs.mine.shape[1]
    upper = place[1] > 0

    def out(member, at, size, rows):
        size = min(size, length - at)
        low, high = rows[:size, 0:128], rows[:size, 128:256]
        refs.mine[member, at : at + size, :] = jnp.where(upper, high, low)
        refs.other[member, at : at + size, :] = jnp.where(upper, low, high).astype(bf16)

    def fetches(at_step):
        slot = at_step % 2
        for i, name in enumerate(DEFERRED):
            shape, _, axis = ATTEND_SAVED[name]
            at = at_step * shape[axis]
            if shape[axis] > PAIR:
                at = pl.multiple_of(at, 128)
            where = [slice(None)] * len(shape)
            where[axis] = pl.ds(at, shape[axis])
            source = getattr(refs, "whole_" + name).at[tuple(where)]
            target = getattr(refs, name).at[slot]
            yield pltpu.make_async_copy(source, target, refs.sem.at[7 * slot + i])

    @pl.when(step == 0)
    def _():
        for copy in fetches(step):
            copy.start()

    backward_feed(refs.e0, refs, refs, refs, refs.feed)
    for copy in fetches(step):
        copy.wait()

    @pl.when(step < pl.num_programs(0) - 1)
    def _():
        for copy in fetches(step + 1):
            copy.start()

    held = {name: getattr(refs, name).at[step % 2] for name in DEFERRED}
    backward_attend(refs, SimpleNamespace(**held), refs, refs.attend, out)
    last = step == pl.num_programs(0) - 1

    @pl.when(jnp.logical_not(last))
    def _():
        refs.early[...] = refs.other[...]

    @pl.when(last)
    def _():
        refs.late[...] = refs.other[...]

    @pl.when(step == pl.num_programs(0) - 1)
    def _():
        emit_halves(refs, place[2])


def column(row):
    return jnp.broadcast_to(row, (8, 256)).T[:, 0:1]


def line(value):
    return jnp.broadcast_to(value, (256, 128)).T[0:1]


def finish(halves, inw, upw, again, ashift, mgain, mshift, outs):
    ga, sa, giw, gib, gow, gob, gm, sm, guw, gub, gdw, gdb = outs

    def block(half, at, count, part):
        start, tail = at + 256 * part, at + 512 * count + ONES * part
        rows = halves[half][start : start + 256, :].astype(f32)
        return rows, halves[half][tail : tail + ONES, :].astype(f32)[0:1]

    gain, shift = column(mgain[...]), column(mshift[...])
    of_gain, of_shift = [], []
    for part in range(8):
        rows, sums = block(0, 0, 4, part)
        lanes = slice(128 * part, 128 * part + 128)
        guw[0, :, lanes] = gain * rows + shift * sums
        gub[:, lanes] = sums
        weight = upw[0, :, lanes].astype(f32)
        of_gain.append(weight * rows)
        of_shift.append(weight * sums)
    gm[...] = line(jnp.sum(tree(jnp.add, of_gain), axis=1, keepdims=True))
    sm[...] = line(jnp.sum(tree(jnp.add, of_shift), axis=1, keepdims=True))
    for part in range(8):
        rows, sums = block(1, 0, 4, part)
        gdw[0, 128 * part : 128 * part + 128, :] = rows.T
        if part < 2:
            gdb[:, 128 * part : 128 * part + 128] = sums
    gain, shift = column(again[...]), column(ashift[...])
    of_gain, of_shift = [], []
    for part in range(8):
        rows, sums = block(part // 4, FEED_HALF, 2, part % 4)
        if part < 6:
            lanes = slice(128 * part, 128 * part + 128)
            giw[0, :, lanes] = gain * rows + shift * sums
            weight = inw[0, :, lanes].astype(f32)
            of_gain.append(weight * rows)
            of_shift.append(weight * sums)
            if part < 2:
                gib[:, lanes] = sums
            elif part >= 4:
                gib[:, 128 * part - 256 : 128 * part - 128] = sums
        else:
            lanes = slice(128 * (part - 6), 128 * (part - 6) + 128)
            gow[0, :, lanes] = rows
            gob[:, lanes] = sums
    ga[...] = line(jnp.sum(tree(jnp.add, of_gain), axis=1, keepdims=True))
    sa[...] = line(jnp.sum(tree(jnp.add, of_shift), axis=1, keepdims=True))


def final_kernel(place, own, far, *refs):
    weights, outs = refs[:6], refs[6:]

    @pl.when(place[2] == 0)
    def _():
        finish((own, far), *weights, outs)

    @pl.when(place[2] != 0)
    def _():
        finish((far, own), *weights, outs)


SMEM = pl.BlockSpec(memory_space=pltpu.SMEM)
VMEM = pl.BlockSpec(memory_space=pltpu.VMEM)
ANY = pl.BlockSpec(memory_space=pl.ANY)


def step_spec(shape, axis=0, held=False):
    def index(i, place):
        at = i + place[0] // PAIR if held else i
        return tuple(at if d == axis else 0 for d in range(len(shape)))

    return pl.BlockSpec(shape, index)


def constant(shape):
    return pl.BlockSpec(shape, lambda i, place: (0,) * len(shape))


def step_arrays(table, steps):
    return {
        name: (
            step_spec(shape, axis),
            jax.ShapeDtypeStruct(
                tuple(n * steps if d == axis else n for d, n in enumerate(shape)), kind
            ),
        )
        for name, (shape, kind, axis) in table.items()
    }


def call(kernel, steps, place, own, far, inputs, outputs, scratch, cost):
    own, far = list(own), list(far)
    count, other = len(own), len(far)
    scratch = dict(scratch, bits=((16, 1024), bf16, 0))
    names = list(inputs) + list(outputs) + list(scratch)

    def run(place, *refs):
        rest = refs[count + other :]
        named = SimpleNamespace(**dict(zip(names, rest)))
        named.own, named.far, named.sem = refs[:count], refs[count : count + other], rest[-1]
        kernel(place, named)

    results = pl.pallas_call(
        run,
        grid_spec=pltpu.PrefetchScalarGridSpec(
            num_scalar_prefetch=1,
            grid=(steps,),
            in_specs=[ANY] * (count + other) + [spec for spec, _ in inputs.values()],
            out_specs=[spec for spec, _ in outputs.values()],
            scratch_shapes=[pltpu.VMEM(shape, kind) for shape, kind, _ in scratch.values()]
            + [pltpu.SemaphoreType.DMA((16,))],
        ),
        out_shape=[shape for _, shape in outputs.values()],
        compiler_params=pltpu.CompilerParams(
            vmem_limit_bytes=VMEM_LIMIT, dimension_semantics=("arbitrary",)
        ),
        cost_estimate=pl.CostEstimate(flops=cost, bytes_accessed=3000000, transcendentals=0),
    )(place, *own, *far, *(operand for _, operand in inputs.values()))
    return dict(zip(outputs, results))


def body(
    tokens,
    cotangent,
    frame_ids,
    attend_gain,
    attend_shift,
    inward_weight,
    inward_bias,
    outward_weight,
    outward_bias,
    mixing_gain,
    mixing_shift,
    up_weight,
    up_bias,
    down_weight,
    down_bias,
):
    section = lax.axis_index("section")
    batch = lax.axis_index("batch")
    batches = lax.axis_size("batch")
    sequences, length, width = tokens.shape
    half = sequences // 2
    steps = half // PAIR
    place = jnp.stack([section * half, section, batch % 2]).astype(jnp.int32)

    def mine(value):
        return lax.dynamic_slice_in_dim(value, section * half, half, 0)

    def across(value):
        return lax.ppermute(value, "section", ((0, 1), (1, 0)))

    def between_cores(value):
        return lax.ppermute(value, "batch", [(b, b ^ 1) for b in range(batches)])

    everyone = ("section", "batch")
    beyond = [1 << bit for bit in range(3, batches.bit_length() - 1)]
    cubes = [
        [s * batches + base + c + 2 * i for s in range(2) for i in range(4)]
        for base in range(0, batches, 8)
        for c in range(2)
    ]

    def exchange(value):
        return lax.all_to_all(value, everyone, 0, 0, tiled=True, axis_index_groups=cubes)

    def partner(value, flip):
        return lax.ppermute(value, "batch", [(b, b ^ flip) for b in range(batches)])

    vectors, half_weights = pl.pallas_call(
        pack_kernel,
        in_specs=[SMEM] + [VMEM] * 10,
        out_specs=[VMEM] * 2,
        out_shape=[
            jax.ShapeDtypeStruct((1, 3072), f32),
            jax.ShapeDtypeStruct((144, 1024), bf16),
        ],
    )(
        place,
        attend_gain,
        attend_shift,
        inward_bias,
        outward_bias,
        mixing_gain,
        mixing_shift,
        up_bias,
        down_bias,
        inward_weight,
        outward_weight,
    )
    own_attend = (vectors, inward_weight[0], outward_weight[0])
    half_feed = pl.pallas_call(
        pack_feed_kernel,
        in_specs=[SMEM] + [VMEM] * 2,
        out_specs=VMEM,
        out_shape=jax.ShapeDtypeStruct((256, 1024), bf16),
    )(place, up_weight, down_weight)
    arrived, half_feed, held_tokens, held_cotangent = lax.optimization_barrier(
        (across(half_weights), half_feed, mine(tokens), mine(cotangent))
    )
    far_attend = (arrived, between_cores(arrived))
    arrived_feed = across(half_feed)

    def whole_frames():
        return constant((sequences, length)), frame_ids

    table = dict(ATTEND_SAVED)
    table.update(middle=BETWEEN["middle"])
    scratch = dict(ATTEND_SCRATCH)
    scratch.update(ATTEND_WEIGHTS)
    scratch.update(second=BETWEEN["second"])
    kept = call(
        attend_kernel,
        steps,
        place,
        own_attend,
        far_attend,
        dict(tokens=(step_spec((PAIR, length, 256)), held_tokens), frames=whole_frames()),
        step_arrays(table, steps),
        scratch,
        18000000000,
    )

    own = [*own_attend, up_weight[0], down_weight[0]]
    arrived_feed, kept["n2"] = lax.optimization_barrier((arrived_feed, kept["n2"]))
    far = [*far_attend, arrived_feed, between_cores(arrived_feed)]

    scratch = {}
    for table in (ATTEND_SCRATCH, BACK_SCRATCH, ATTEND_SAVED, BETWEEN, GELU_SAVED, WEIGHTS, ACC):
        scratch.update(table)
    for name in FEED_WEIGHTS:
        scratch["low_" + name] = WEIGHTS[name]
    scratch.update(e=((BOTH, 256), bf16, 0), low_second=((BOTH, 256), bf16, 0))
    outputs = {"low_" + name: pair for name, pair in step_arrays(GELU_SAVED, steps).items()}
    outputs.update(step_arrays(dict(e0=((BOTH, 256), bf16, 0)), steps))
    outputs.update(
        mine=(
            step_spec((PAIR, length, 128), 0, True),
            jax.ShapeDtypeStruct((sequences, length, 128), bf16),
        ),
        other=(
            step_spec((PAIR, length, 128)),
            jax.ShapeDtypeStruct((half, length, 128), bf16),
        ),
        keep=(constant((WIRE, 128)), jax.ShapeDtypeStruct((WIRE, 128), bf16)),
        send=(constant((WIRE, 128)), jax.ShapeDtypeStruct((WIRE, 128), bf16)),
    )
    results = call(
        middle_kernel,
        steps,
        place,
        own,
        far,
        dict(
            low_n2=(step_spec((BOTH, 256)), kept["n2"]),
            low_middle=(step_spec((BOTH, 256)), kept["middle"]),
            cotangent=(step_spec((PAIR, length, 256)), held_cotangent),
            frames=whole_frames(),
        ),
        outputs,
        scratch,
        72000000000,
    )
    kept.update(act=results["low_act"], dg=results["low_dg"])
    out_own = results["mine"]

    chunk = WIRE // 8

    def sum_cores(keep, send):
        total = keep.astype(f32) + between_cores(send).astype(f32)
        return total.astype(bf16).reshape(8, chunk, 128)

    def chunk_of(parts):
        total = jnp.sum(parts.astype(f32), axis=0).astype(bf16)
        for flip in beyond:
            total = lax.optimization_barrier(total)
            total = (total.astype(f32) + partner(total, flip).astype(f32)).astype(bf16)
        return total

    upper_parts, e0 = lax.optimization_barrier(
        (sum_cores(results["keep"], results["send"]), results["e0"])
    )
    upper_parts = exchange(upper_parts)
    out_arrived = across(results["other"])

    table = dict(ATTEND_SAVED)
    table.update(GELU_SAVED)
    inputs = {
        name: (spec, kept[name]) for name, (spec, _) in step_arrays(table, steps).items()
    }
    inputs.update(e0=(step_spec((BOTH, 256)), e0))
    for name in DEFERRED:
        inputs["whole_" + name] = (ANY, inputs.pop(name)[1])
    scratch = dict(BACK_SCRATCH)
    scratch.update(WEIGHTS)
    scratch.update(ACC)
    scratch.update(
        {name: ((2,) + ATTEND_SAVED[name][0], bf16, 0) for name in DEFERRED}
    )
    scratch.update(other=((PAIR, length, 128), bf16, 0))
    results = call(
        back_kernel,
        steps,
        place,
        own,
        far,
        inputs,
        dict(
            mine=(
                step_spec((PAIR, length, 128), 0, True),
                jax.ShapeDtypeStruct((sequences, length, 128), f32),
            ),
            early=(
                pl.BlockSpec((PAIR, length, 128), lambda i, p: (jnp.minimum(i, steps - 2), 0, 0)),
                jax.ShapeDtypeStruct((half - PAIR, length, 128), bf16),
            ),
            late=(
                constant((PAIR, length, 128)),
                jax.ShapeDtypeStruct((PAIR, length, 128), bf16),
            ),
            keep=(constant((WIRE, 128)), jax.ShapeDtypeStruct((WIRE, 128), bf16)),
            send=(constant((WIRE, 128)), jax.ShapeDtypeStruct((WIRE, 128), bf16)),
        ),
        scratch,
        40000000000,
    )
    upper_parts, out_arrived, grad_own, grad_early, grad_late, keep, send = (
        lax.optimization_barrier(
            (
                upper_parts,
                out_arrived,
                results["mine"],
                results["early"],
                results["late"],
                results["keep"],
                results["send"],
            )
        )
    )
    late_arrived = across(grad_late)
    lower_parts, late_arrived = lax.optimization_barrier((sum_cores(keep, send), late_arrived))
    lower_parts = exchange(lower_parts)
    early_arrived = across(grad_early)
    upper_chunk = chunk_of(upper_parts)

    ours = (jnp.arange(sequences) // half == section)[None, :, None]

    def assemble(held, arrived):
        arrived = jnp.concatenate([arrived, arrived], axis=0).astype(held.dtype)
        value = jnp.where(ours, held.transpose(1, 0, 2), arrived.transpose(1, 0, 2))
        return with_layout_constraint(value, Layout((0, 1, 2)))

    layer_out = assemble(out_own, out_arrived)
    lower_chunk, layer_out, early_arrived = lax.optimization_barrier(
        (chunk_of(lower_parts), layer_out, early_arrived)
    )
    spread = (4, chunk, 128)
    own_half = exchange(
        jnp.concatenate(
            [jnp.broadcast_to(lower_chunk, spread), jnp.broadcast_to(upper_chunk, spread)]
        )
    )
    input_grad = assemble(grad_own, jnp.concatenate([early_arrived, late_arrived], axis=0))
    own_half, input_grad = lax.optimization_barrier((own_half, input_grad))
    far_half = between_cores(own_half)

    grads = (
        (1, 256),
        (1, 256),
        (1, 256, 768),
        (1, 512),
        (1, 256, 256),
        (1, 256),
        (1, 256),
        (1, 256),
        (1, 256, 1024),
        (1, 1024),
        (1, 1024, 256),
        (1, 256),
    )
    finals = pl.pallas_call(
        final_kernel,
        in_specs=[SMEM] + [VMEM] * 8,
        out_specs=[VMEM] * 12,
        out_shape=[jax.ShapeDtypeStruct(shape, f32) for shape in grads],
        compiler_params=pltpu.CompilerParams(vmem_limit_bytes=VMEM_LIMIT),
    )(
        place,
        own_half.reshape(WIRE, 128),
        far_half.reshape(WIRE, 128),
        inward_weight,
        up_weight,
        attend_gain,
        attend_shift,
        mixing_gain,
        mixing_shift,
    )
    return (layer_out.transpose(1, 0, 2), input_grad.transpose(1, 0, 2), *finals)


def solution(mesh):
    spread = P("section", None)
    deep = P("section", None, None)
    weights = (
        spread,
        spread,
        deep,
        spread,
        deep,
        spread,
        spread,
        spread,
        deep,
        spread,
        deep,
        spread,
    )
    rows = P("batch", None, None)
    return jax.shard_map(
        body,
        mesh=mesh,
        in_specs=(rows, rows, P("batch", None)) + weights,
        out_specs=(P("batch", None, "section"),) * 2 + weights,
        check_vma=False,
    )
```

```python
import functools
from types import SimpleNamespace

import jax
import jax.numpy as jnp
from jax import lax
from jax.experimental import pallas as pl
from jax.experimental.layout import Layout, with_layout_constraint
from jax.experimental.pallas import tpu as pltpu
from jax.sharding import PartitionSpec as P

HEADS = 4
WHOLE_FRAME = 17

epsilon = 1e-05
masked_value = -1e30
log2e = 1.4426950408889634

PAIR = 2
LIVE = 368
ROWS = 384
BOTH = PAIR * ROWS
USED = BOTH - ROWS + LIVE
ONES = 16
STEP = 48
CHUNKS = tuple((at, min(STEP, LIVE - at)) for at in range(0, LIVE, STEP))
MEMBERS = tuple(range(PAIR))
TILES = ((0, 144, 0), (128, 272, 128), (256, 368, 256))
STACK = (0, 144, 416)
STACKED = 784

bf16 = jnp.bfloat16
f32 = jnp.float32


def dot(left, right):
    return jnp.dot(left, right, preferred_element_type=f32)


def dot_upper(left, right):
    return lax.dot_general(left, right, (((1,), (1,)), ((), ())), preferred_element_type=f32)


def gelu_pair(value):
    half = 0.5 + 0.5 * lax.erf(value * 0.7071067811865476)
    bell = jnp.exp2(value * value * (-0.5 * log2e) - 1.3257480647361595)
    return value * half, half + value * bell


def tree(op, parts):
    parts = list(parts)
    while len(parts) > 1:
        pairs = [op(a, b) for a, b in zip(parts[0::2], parts[1::2])]
        parts = pairs + parts[len(parts) // 2 * 2 :]
    return parts[0]


def eights(value):
    return [value[at : at + 8] for at in range(0, value.shape[0], 8)]


def twice(stat):
    return jnp.concatenate([stat, stat], axis=1)


def row_mean(value):
    mean = jnp.mean(value, axis=-1, keepdims=True)
    return jnp.broadcast_to(mean, (value.shape[0], 128))


def normalize(load, T, scales, store):
    for _, _, _, rows in chunks():
        T.mean[rows, :] = row_mean(load(rows))
    for _, _, _, rows in chunks():
        center = load(rows) - twice(T.mean[rows, :])
        T.spread[rows, :] = row_mean(center * center)
    for _, _, _, rows in chunks():
        scale = lax.rsqrt(T.spread[rows, :] + epsilon)
        scales[rows, :] = scale.astype(bf16)
        store(rows, (load(rows) - twice(T.mean[rows, :])) * twice(scale))


def norm_back(gain, g, normed, scales, T, store):
    for _, _, _, rows in chunks():
        gn = g[rows, :] * gain
        T.mean[rows, :] = row_mean(gn)
        T.slope[rows, :] = row_mean(gn * normed[rows, :].astype(f32))
    for chunk in chunks():
        rows = chunk[3]
        gn = g[rows, :] * gain - twice(T.mean[rows, :])
        back = gn - normed[rows, :].astype(f32) * twice(T.slope[rows, :])
        store(chunk, twice(scales[rows, :].astype(f32)) * back)


def masked_pair(value, head):
    lane = lax.broadcasted_iota(jnp.int32, value.shape, 1)
    keep = (lane < 64) if head % 2 == 0 else (lane >= 64)
    return jnp.where(keep, value, jnp.zeros_like(value))


def pair_lanes(head):
    return slice(128 * (head // 2), 128 * (head // 2) + 128)


def two_heads(ref, p, rows):
    value = ref[rows, 128 * p : 128 * p + 128]
    return jnp.concatenate([masked_pair(value, 0), masked_pair(value, 1)], axis=0)


def column_of(t, side):
    return slice(256 * t + 128 * side, 256 * t + 128 * side + 128)


def stack_of(t):
    return slice(STACK[t], STACK[t] + TILES[t][1])


def of(member, start, stop):
    return slice(member * ROWS + start, member * ROWS + stop)


def chunks():
    for member in MEMBERS:
        for at, size in CHUNKS:
            yield member, at, size, pl.ds(member * ROWS + at, size)


def clear_tails(*refs):
    for ref in refs:
        for member in MEMBERS:
            rows = of(member, LIVE, ROWS)
            ref[rows, :] = jnp.zeros((ROWS - LIVE,) + ref.shape[1:], ref.dtype)


def forward_attend(x, lines, W, S, T):
    vec = W.vec

    def first(rows, n):
        S.n1[rows, :] = n.astype(bf16)
        T.a[rows, :] = (n * vec[:, 0:256] + vec[:, 256:512]).astype(bf16)

    normalize(lambda rows: x[rows, :].astype(f32), T, S.r1, first)
    clear_tails(S.n1)
    a = T.a[0:USED, :]
    packed = dot(a, W.inw[...])
    T.k[0:USED, :] = packed[:, 256:512].astype(bf16)
    S.q[0:USED, :] = (packed[:, 0:256] + vec[:, 512:768]).astype(bf16)
    S.v[0:USED, :] = (packed[:, 512:768] + vec[:, 768:1024]).astype(bf16)
    clear_tails(T.k, S.q, S.v)
    for member in MEMBERS:
        frames = lines[member]
        length = frames.shape[1]
        first = jnp.sum((frames == 0).astype(f32), axis=1, keepdims=True).astype(jnp.int32)
        last = jnp.minimum(first - 1 + WHOLE_FRAME * frames, length - 1)
        T.last[:, :] = jnp.full((1, ROWS), length - 1, jnp.int32)
        T.last[:, 0:length] = last
        for t, (at, stop, sure) in enumerate(TILES):
            keys = lax.broadcasted_iota(jnp.int32, (stop - sure, 128), 0) + sure
            seen = keys <= T.last[:, at : at + 128]
            T.mask[member, t, 0 : stop - sure, :] = jnp.where(seen, 0.0, masked_value)
    power = 0.125 * log2e
    units = [(p, member) for p in range(2) for member in MEMBERS]

    def scores(u):
        p, member = units[u]
        for t, (at, stop, sure) in enumerate(TILES):
            lanes = slice(256 * t, 256 * t + 256)
            both = dot_upper(
                T.k[of(member, 0, stop), 128 * p : 128 * p + 128],
                two_heads(S.q, p, of(member, at, at + 128)),
            )
            if sure:
                T.s[u % 3, 0:sure, lanes] = both[0:sure]
            mask = twice(T.mask[member, t, 0 : stop - sure, :])
            T.s[u % 3, sure:stop, lanes] = both[sure:stop] + mask

    def strips(u, t, side):
        for start in range(0, TILES[t][1], 16):
            yield start, T.s[u % 3, start : start + 16, column_of(t, side)]

    columns = [(t, side) for t in range(3) for side in range(2)]

    def peaks(u):
        for t, side in columns:
            tops = [tree(jnp.maximum, eights(value)) for _, value in strips(u, t, side)]
            peak = jnp.max(tree(jnp.maximum, tops), axis=0, keepdims=True)
            T.peak[u % 3, :, column_of(t, side)] = peak * power

    def raises(u):
        for t, side in columns:
            lanes = column_of(t, side)
            peak = T.peak[u % 3, :, lanes]
            sums = []
            for start, value in strips(u, t, side):
                value = jnp.exp2(value * power - peak)
                T.s[u % 3, start : start + 16, lanes] = value
                sums.append(value[0:8] + value[8:16])
            total = jnp.sum(tree(jnp.add, sums), axis=0, keepdims=True)
            T.share[u % 3, :, lanes] = 1.0 / total

    def shares(u):
        p, member = units[u]
        for t, side in columns:
            lanes = column_of(t, side)
            share = T.share[u % 3, :, lanes]
            for start in range(0, TILES[t][1], 16):
                value = T.s[u % 3, start : start + 16, lanes] * share
                rows = slice(STACK[t] + start, STACK[t] + start + 16)
                S.pT[member, p, rows, 128 * side : 128 * side + 128] = value.astype(bf16)

    def mix(u):
        p, member = units[u]
        for t, (at, stop, _) in enumerate(TILES):
            both = dot(
                T.vT[128 * p : 128 * p + 128, of(member, 0, stop)],
                S.pT[member, p, stack_of(t), :],
            )
            for side in range(2):
                feats = slice(128 * p + 64 * side, 128 * p + 64 * side + 64)
                value = both[64 * side : 64 * side + 64, 128 * side : 128 * side + 128]
                S.mT[feats, of(member, at, at + 128)] = value.astype(bf16)

    scores(0)
    T.vT[...] = S.v[...].T
    peaks(0)
    scores(1)
    S.kT[...] = T.k[...].T
    raises(0)
    peaks(1)
    for u in range(len(units)):
        if u + 2 < len(units):
            scores(u + 2)
        shares(u)
        if u + 1 < len(units):
            raises(u + 1)
        if u + 2 < len(units):
            peaks(u + 2)
        mix(u)
    S.mT[256 : 256 + ONES, :] = jnp.ones((ONES, BOTH), bf16)
    mixed = S.mT[0:256, :].T
    T.f[...] = dot(mixed[0:USED], W.outw[...])
    for _, _, _, rows in chunks():
        S.middle[rows, :] = x[rows, :].astype(f32) + (T.f[rows, :] + vec[:, 1024:1280])

    def second(rows, n):
        S.n2[rows, :] = n.astype(bf16)
        S.second[rows, :] = (n * vec[:, 1280:1536] + vec[:, 1536:1792]).astype(bf16)

    normalize(lambda rows: S.middle[rows, :], T, S.r2, second)
    clear_tails(S.n2, S.second)


def forward_feed(W, S, T, out):
    vec = W.vec
    second = S.second[0:USED, :]

    T.g[...] = dot(second, W.upw[...])
    for c in range(4):
        cols = slice(256 * c, 256 * c + 256)
        for member, at, size, rows in chunks():
            bias = vec[:, 1792 + 256 * c : 2048 + 256 * c]
            act, slope = gelu_pair(T.g[rows, cols] + bias)
            S.act[rows, cols] = act.astype(bf16)
            S.dg[rows, cols] = slope.astype(bf16)
    clear_tails(S.act, S.dg)
    T.g[:, 0:256] = dot(S.act[0:USED, :], W.dnw[...])
    for member, at, size, rows in chunks():
        out(member, at, size, S.middle[rows, :] + (T.g[rows, 0:256] + vec[:, 2816:3072]))


def backward_feed(e_ref, W, S, T, acc):
    vec = W.vec
    e = e_ref[0:USED, :]
    eT = e_ref[...].T
    T.n2T[0:256, :] = S.n2[...].T

    T.g[...] = dot_upper(e, W.dnw[...])
    downs = dot(eT, S.act[...])
    for c in range(4):
        cols = slice(256 * c, 256 * c + 256)
        acc[4 + c, 0:256, :] += downs[:, cols]
        for member, at, size, rows in chunks():
            slope = S.dg[rows, cols].astype(f32)
            T.gr[rows, cols] = (T.g[rows, cols] * slope).astype(bf16)
    T.g[:, 0:256] = dot_upper(T.gr[0:USED, :], W.upw[...])
    ups = dot(T.n2T[...], T.gr[...])
    for c in range(4):
        acc[c] += ups[:, 256 * c : 256 * c + 256]
    columns = []

    def middle(chunk, back):
        rows = chunk[3]
        incoming = e_ref[rows, :].astype(f32)
        columns.append(tree(jnp.add, eights(incoming)))
        middle = incoming + back
        T.gmiddle[rows, :] = middle
        T.gp[rows, :] = middle.astype(bf16)

    norm_back(vec[:, 1280:1536], T.g.at[:, 0:256], S.n2, S.r2, T, middle)
    acc[4, 256 : 256 + ONES, :] += jnp.sum(tree(jnp.add, columns), axis=0, keepdims=True)


def backward_attend(W, S, T, acc, out):
    vec = W.vec
    gp = T.gp[...]
    T.gm[0:USED, :] = dot_upper(gp[0:USED], W.outw[...]).astype(bf16)
    T.n1T[0:256, :] = S.n1[...].T
    gmT = dot_upper(W.outw[...], gp)
    for h in range(HEADS):
        feats = slice(64 * h, 64 * h + 64)
        product = gmT[feats] * S.mT[feats, :].astype(f32)
        T.inner[h : h + 1, :] = jnp.sum(product, axis=0, keepdims=True)
    units = [(p, member) for p in range(2) for member in MEMBERS]

    def slopes(u):
        p, member = units[u]
        for t, (at, stop, _) in enumerate(TILES):
            queries = of(member, at, at + 128)
            gprobs = dot_upper(
                S.v[of(member, 0, stop), 128 * p : 128 * p + 128], two_heads(T.gm, p, queries)
            )
            probs = S.pT[member, p, stack_of(t), :].astype(f32)
            inner = [T.inner[2 * p + side : 2 * p + side + 1, queries] for side in range(2)]
            slope = probs * (gprobs - jnp.concatenate(inner, axis=1))
            T.ds[u % 2, stack_of(t), :] = slope.astype(bf16)

    def gather(parts, scale=None):
        start = 0
        for t, (_, stop, _) in enumerate(TILES):
            value = tree(jnp.add, [part[start:stop] for part in parts[t:]])
            value = value if scale is None else value * scale
            yield start, stop, value.astype(bf16)
            start = stop

    def products(u):
        p, member = units[u]
        gk, gv = [], []
        for t, (at, stop, _) in enumerate(TILES):
            queries = of(member, at, at + 128)
            ds = T.ds[u % 2, stack_of(t), :]
            gk.append(dot(ds, two_heads(S.q, p, queries)))
            gv.append(dot(S.pT[member, p, stack_of(t), :], two_heads(T.gm, p, queries)))
            both = dot(S.kT[128 * p : 128 * p + 128, of(member, 0, stop)], ds) * 0.125
            for side in range(2):
                feats = slice(128 * p + 64 * side, 128 * p + 64 * side + 64)
                value = both[64 * side : 64 * side + 64, 128 * side : 128 * side + 128]
                T.gqT[feats, queries] = value.astype(bf16)
        for start, stop, value in gather(gk, 0.125):
            T.gqkv[of(member, start, stop), 256 + 128 * p : 384 + 128 * p] = value
        for start, stop, value in gather(gv):
            T.gqkv[of(member, start, stop), 512 + 128 * p : 640 + 128 * p] = value

    slopes(0)
    acc[3] += dot(S.mT[...], gp)
    for u in range(len(units)):
        if u + 1 < len(units):
            slopes(u + 1)
        products(u)
    T.gqkv[:, 0:256] = T.gqT[...].T
    T.g[:, 0:256] = dot_upper(T.gqkv[0:USED, :], W.inw[...])
    ins = dot(T.n1T[...], T.gqkv[...])
    for b in range(3):
        acc[b] += ins[:, 256 * b : 256 * b + 256]

    def finish(chunk, back):
        member, at, size, rows = chunk
        out(member, at, size, T.gmiddle[rows, :] + back)

    norm_back(vec[:, 0:256], T.g.at[:, 0:256], S.n1, S.r1, T, finish)


ATTEND_SAVED = dict(
    n1=((BOTH, 256), bf16, 0),
    r1=((BOTH, 128), bf16, 0),
    v=((BOTH, 256), bf16, 0),
    kT=((256, BOTH), bf16, 1),
    q=((BOTH, 256), bf16, 0),
    pT=((PAIR, 2, STACKED, 256), bf16, 0),
    mT=((256 + ONES, BOTH), bf16, 1),
    n2=((BOTH, 256), bf16, 0),
    r2=((BOTH, 128), bf16, 0),
)
BETWEEN = dict(second=((BOTH, 256), bf16, 0), middle=((BOTH, 256), f32, 0))
GELU_SAVED = dict(act=((BOTH, 1024), bf16, 0), dg=((BOTH, 1024), bf16, 0))
ATTEND_SCRATCH = dict(
    a=((BOTH, 256), bf16, 0),
    k=((BOTH, 256), bf16, 0),
    vT=((256, BOTH), bf16, 1),
    last=((1, ROWS), jnp.int32, 0),
    mask=((PAIR, 3, 144, 128), f32, 0),
    s=((3, LIVE, 2 * ROWS), f32, 0),
    peak=((3, 1, 2 * ROWS), f32, 0),
    share=((3, 1, 2 * ROWS), f32, 0),
    mean=((BOTH, 128), f32, 0),
    spread=((BOTH, 128), f32, 0),
    f=((USED, 256), f32, 0),
    x=((BOTH, 256), bf16, 0),
)
BACK_SCRATCH = dict(
    mean=((BOTH, 128), f32, 0),
    slope=((BOTH, 128), f32, 0),
    g=((USED, 1024), f32, 0),
    gr=((BOTH, 1024), bf16, 0),
    gp=((BOTH, 256), bf16, 0),
    gmiddle=((BOTH, 256), f32, 0),
    n1T=((256 + ONES, BOTH), bf16, 1),
    n2T=((256 + ONES, BOTH), bf16, 1),
    gm=((BOTH, 256), bf16, 0),
    inner=((8, BOTH), f32, 0),
    ds=((2, STACKED, 256), bf16, 0),
    gqT=((256, BOTH), bf16, 0),
    gqkv=((BOTH, 768), bf16, 0),
)
ATTEND_WEIGHTS = dict(
    vec=((1, 3072), f32, 0),
    inw=((256, 768), bf16, 0),
    outw=((256, 256), bf16, 0),
)
WEIGHTS = dict(
    upw=((256, 1024), bf16, 0),
    dnw=((1024, 256), bf16, 0),
)
FEED_WEIGHTS = dict(WEIGHTS, vec=ATTEND_WEIGHTS["vec"])
WEIGHTS = dict(ATTEND_WEIGHTS, **WEIGHTS)
ACC = dict(
    feed=((8, 256 + ONES, 256), f32, 0),
    attend=((4, 256 + ONES, 256), f32, 0),
)
FEED_HALF = 8 * 256 + 128
ATTEND_HALF = 4 * 256 + 128
WIRE = FEED_HALF + ATTEND_HALF
VMEM_LIMIT = 62 * 1024 * 1024


def load_padded(ref, member, source, length):
    whole = length // 16 * 16
    ref[of(member, whole, ROWS), :] = jnp.zeros((ROWS - whole, 256), bf16)
    ref[of(member, 0, length), :] = source[...]


def fetch_weights(refs, layer, place, attend, feed=None, meanwhile=None):
    vec, inw, outw = attend
    core = place[2]

    def run(pairs):
        copies = [
            pltpu.make_async_copy(source, target, refs.sem.at[i])
            for i, (source, target) in enumerate(pairs)
        ]
        for copy in copies:
            copy.start()
        if meanwhile is not None:
            meanwhile()
        for copy in copies:
            copy.wait()

    @pl.when(place[1] == layer)
    def _():
        pairs = [(refs.own[0], vec)]
        if inw is not None:
            pairs += [(refs.own[1], inw), (refs.own[2], outw)]
        if feed is not None:
            pairs += list(zip(refs.own[3:], feed))
        run(pairs)

    @pl.when(place[1] != layer)
    def _():
        pairs = [(refs.far[0].at[128:144, :], refs.bits)]
        if inw is not None:
            for i in range(2):
                at = (core if i == 0 else 1 - core) * 128
                rows = pl.ds(pl.multiple_of(at, 128), 128)
                pairs.append((refs.far[i].at[0:128, 0:768], inw.at[rows, :]))
                pairs.append((refs.far[i].at[0:128, 768:1024], outw.at[rows, :]))
        if feed is not None:
            upw, dnw = feed
            for i in range(2):
                part = refs.far[2 + i]
                at = core if i == 0 else 1 - core
                rows = pl.ds(pl.multiple_of(at * 128, 128), 128)
                pairs.append((part.at[0:128, :], upw.at[rows, :]))
                for j in range(4):
                    rows = pl.ds(pl.multiple_of(at * 512 + 128 * j, 128), 128)
                    lanes = slice(256 * j, 256 * j + 256)
                    pairs.append((part.at[128:256, lanes], dnw.at[rows, :]))
        run(pairs)
        parts = refs.bits[...].astype(f32)
        for j in range(3):
            value = parts[j : j + 1] + parts[3 + j : 4 + j] + parts[6 + j : 7 + j]
            vec[:, 1024 * j : 1024 * j + 1024] = value


def emit_rows(target, at, blocks):
    tail = at + 512 * len(blocks)
    target[tail : tail + 128, :] = jnp.zeros((128, 128), target.dtype)
    for j, block in enumerate(blocks):
        for side in range(2):
            lanes = slice(128 * side, 128 * side + 128)
            part = 2 * j + side
            target[at + 256 * part : at + 256 * part + 256, :] = block[0:256, lanes].astype(
                target.dtype
            )
            target[tail + ONES * part : tail + ONES * part + ONES, :] = block[
                256 : 256 + ONES, lanes
            ].astype(target.dtype)


def emit_half(target, at, half, acc):
    emit_rows(target, at, [acc.feed.at[4 * half + b] for b in range(4)])
    emit_rows(target, at + FEED_HALF, [acc.attend.at[2 * half + b] for b in range(2)])


def emit_halves(refs, core):
    for half in range(2):

        @pl.when(core == half)
        def _(half=half):
            emit_half(refs.keep, 0, half, refs)
            emit_half(refs.send, 0, 1 - half, refs)


def pack_kernel(*refs):
    vec, half = refs[-2:]
    inw, outw = refs[8:10]
    at = 0
    for ref in refs[:8]:
        vec[:, at : at + ref.shape[1]] = ref[...]
        at += ref.shape[1]
    rows = pl.ds(pl.multiple_of(lax.axis_index("batch") % 2 * 128, 128), 128)
    half[0:128, 0:768] = inw[0, rows, :]
    half[0:128, 768:1024] = outw[0, rows, :]
    rest = jnp.concatenate([vec[:, 1024 * j : 1024 * j + 1024] for j in range(3)], axis=0)
    parts = []
    for _ in range(3):
        part = rest.astype(bf16).astype(f32)
        parts.append(part)
        rest = rest - part
    parts.append(jnp.zeros((7, 1024), f32))
    half[128:144, :] = jnp.concatenate(parts, axis=0).astype(bf16)


def pack_feed_kernel(upw, dnw, half):
    core = lax.axis_index("batch") % 2
    half[0:128, :] = upw[0, pl.ds(pl.multiple_of(core * 128, 128), 128), :]
    for j in range(4):
        rows = pl.ds(pl.multiple_of(core * 512 + 128 * j, 128), 128)
        half[128:256, 256 * j : 256 * j + 256] = dnw[0, rows, :]


def zero(refs):
    for ref in refs:
        ref[...] = jnp.zeros(ref.shape, ref.dtype)


def set_ones(*refs):
    for ref in refs:
        ref[256 : 256 + ONES, :] = jnp.ones((ONES, BOTH), bf16)


def attend_kernel(place, refs):
    step = pl.program_id(0)

    @pl.when(step == 0)
    def _():
        fetch_weights(refs, 0, place, (refs.vec, refs.inw, refs.outw))

    length = refs.frames.shape[1]
    lines = []
    for member in MEMBERS:
        load_padded(refs.x, member, refs.tokens.at[member], length)
        lines.append(refs.frames[pl.ds(place[0] + PAIR * step + member, 1), :])
    forward_attend(refs.x, lines, refs, refs, refs)


def middle_kernel(place, refs):
    step = pl.program_id(0)

    @pl.when(step == 0)
    def _():
        def clear():
            zero([refs.feed, refs.attend])
            clear_tails(refs.gqkv, refs.gr, refs.gp, refs.gm, refs.x, refs.low_second)
            set_ones(refs.n1T, refs.n2T)

        held = (refs.low_vec, None, None)
        fetch_weights(refs, 0, place, held, (refs.low_upw, refs.low_dnw), clear)
        held = (refs.vec, refs.inw, refs.outw)
        fetch_weights(refs, 1, place, held, (refs.upw, refs.dnw))

    length = refs.frames.shape[1]
    upper = place[1] > 0
    lower = SimpleNamespace(upw=refs.low_upw, dnw=refs.low_dnw, vec=refs.low_vec)
    below = SimpleNamespace(
        second=refs.low_second, middle=refs.low_middle, act=refs.low_act, dg=refs.low_dg
    )

    def out_lower(member, at, size, rows):
        refs.x[of(member, at, at + size), :] = rows.astype(bf16)

    def out(member, at, size, rows):
        size = min(size, length - at)
        rows = rows[:size].astype(bf16)
        low, high = rows[:, 0:128], rows[:, 128:256]
        refs.mine[member, at : at + size, :] = jnp.where(upper, high, low)
        refs.other[member, at : at + size, :] = jnp.where(upper, low, high)

    def out_back(member, at, size, rows):
        refs.e0[of(member, at, at + size), :] = rows.astype(bf16)

    lines = []
    for member in MEMBERS:
        load_padded(refs.e, member, refs.cotangent.at[member], length)
        lines.append(refs.frames[pl.ds(place[0] + PAIR * step + member, 1), :])
    for member, at, size, rows in chunks():
        n = refs.low_n2[rows, :].astype(f32)
        second = n * refs.low_vec[:, 1280:1536] + refs.low_vec[:, 1536:1792]
        refs.low_second[rows, :] = second.astype(bf16)
    forward_feed(lower, below, refs, out_lower)
    forward_attend(refs.x, lines, refs, refs, refs)
    forward_feed(refs, refs, refs, out)
    backward_feed(refs.e, refs, refs, refs, refs.feed)
    clear_tails(refs.e0)
    backward_attend(refs, refs, refs, refs.attend, out_back)

    @pl.when(step == pl.num_programs(0) - 1)
    def _():
        emit_halves(refs, place[2])


DEFERRED = ("v", "kT", "q", "pT", "mT", "n1", "r1")


def back_kernel(place, refs):
    step = pl.program_id(0)

    @pl.when(step == 0)
    def _():
        def clear():
            zero([refs.feed, refs.attend])
            clear_tails(refs.gqkv, refs.gr, refs.gp, refs.gm)
            set_ones(refs.n1T, refs.n2T)

        held = (refs.vec, refs.inw, refs.outw)
        fetch_weights(refs, 0, place, held, (refs.upw, refs.dnw), clear)

    length = refs.mine.shape[1]
    upper = place[1] > 0

    def out(member, at, size, rows):
        size = min(size, length - at)
        low, high = rows[:size, 0:128], rows[:size, 128:256]
        refs.mine[member, at : at + size, :] = jnp.where(upper, high, low)
        refs.other[member, at : at + size, :] = jnp.where(upper, low, high).astype(bf16)

    def fetches(at_step):
        slot = at_step % 2
        for i, name in enumerate(DEFERRED):
            shape, _, axis = ATTEND_SAVED[name]
            at = at_step * shape[axis]
            if shape[axis] > PAIR:
                at = pl.multiple_of(at, 128)
            where = [slice(None)] * len(shape)
            where[axis] = pl.ds(at, shape[axis])
            source = getattr(refs, "whole_" + name).at[tuple(where)]
            target = getattr(refs, name).at[slot]
            yield pltpu.make_async_copy(source, target, refs.sem.at[7 * slot + i])

    @pl.when(step == 0)
    def _():
        for copy in fetches(step):
            copy.start()

    backward_feed(refs.e0, refs, refs, refs, refs.feed)
    for copy in fetches(step):
        copy.wait()

    @pl.when(step < pl.num_programs(0) - 1)
    def _():
        for copy in fetches(step + 1):
            copy.start()

    held = {name: getattr(refs, name).at[step % 2] for name in DEFERRED}
    backward_attend(refs, SimpleNamespace(**held), refs, refs.attend, out)
    last = step == pl.num_programs(0) - 1

    @pl.when(jnp.logical_not(last))
    def _():
        refs.early[...] = refs.other[...]

    @pl.when(last)
    def _():
        refs.late[...] = refs.other[...]

    @pl.when(step == pl.num_programs(0) - 1)
    def _():
        emit_halves(refs, place[2])


def column(row):
    return jnp.broadcast_to(row, (8, 256)).T[:, 0:1]


def line(value):
    return jnp.broadcast_to(value, (256, 128)).T[0:1]


def finish(halves, weights, vectors, small, large, copies):
    again, ashift, mgain, mshift = vectors
    ga, sa, gib, gob, gm, sm, gub, gdb = small
    giw, gow, guw, gdw = large
    inw, upw = weights
    fetch_inw, fetch_upw, send_giw, send_gow, send_guw, send_gdw = copies

    def block(half, at, count, part):
        start, tail = at + 256 * part, at + 512 * count + ONES * part
        rows = halves[half][start : start + 256, :].astype(f32)
        return rows, halves[half][tail : tail + ONES, :].astype(f32)[0:1]

    for part in range(8):
        rows, sums = block(1, 0, 4, part)
        gdw[0, 128 * part : 128 * part + 128, :] = rows.T
        if part < 2:
            gdb[:, 128 * part : 128 * part + 128] = sums
    send_gdw.start()
    fetch_upw.wait()
    gain, shift = column(mgain[...]), column(mshift[...])
    of_gain, of_shift = [], []
    for part in range(8):
        rows, sums = block(0, 0, 4, part)
        lanes = slice(128 * part, 128 * part + 128)
        guw[0, :, lanes] = gain * rows + shift * sums
        gub[:, lanes] = sums
        weight = upw[0, :, lanes].astype(f32)
        of_gain.append(weight * rows)
        of_shift.append(weight * sums)
    send_guw.start()
    gm[...] = line(jnp.sum(tree(jnp.add, of_gain), axis=1, keepdims=True))
    sm[...] = line(jnp.sum(tree(jnp.add, of_shift), axis=1, keepdims=True))
    fetch_inw.wait()
    gain, shift = column(again[...]), column(ashift[...])
    of_gain, of_shift = [], []
    for part in range(8):
        rows, sums = block(part // 4, FEED_HALF, 2, part % 4)
        if part < 6:
            lanes = slice(128 * part, 128 * part + 128)
            giw[0, :, lanes] = gain * rows + shift * sums
            weight = inw[0, :, lanes].astype(f32)
            of_gain.append(weight * rows)
            of_shift.append(weight * sums)
            if part < 2:
                gib[:, lanes] = sums
            elif part >= 4:
                gib[:, 128 * part - 256 : 128 * part - 128] = sums
        else:
            lanes = slice(128 * (part - 6), 128 * (part - 6) + 128)
            gow[0, :, lanes] = rows
            gob[:, lanes] = sums
    send_giw.start()
    send_gow.start()
    ga[...] = line(jnp.sum(tree(jnp.add, of_gain), axis=1, keepdims=True))
    sa[...] = line(jnp.sum(tree(jnp.add, of_shift), axis=1, keepdims=True))
    for copy in (send_giw, send_gow, send_guw, send_gdw):
        copy.wait()


def final_kernel(place, own, far, inw, upw, again, ashift, mgain, mshift, *refs):
    ga, sa, giw, gib, gow, gob, gm, sm, guw, gub, gdw, gdb = refs[:12]
    *held, sem = refs[12:]
    pairs = [(inw, held[0]), (upw, held[1])]
    pairs += list(zip(held[2:], (giw, gow, guw, gdw)))
    copies = [pltpu.make_async_copy(a, b, sem.at[i]) for i, (a, b) in enumerate(pairs)]
    copies[0].start()
    copies[1].start()
    vectors = (again, ashift, mgain, mshift)
    small = (ga, sa, gib, gob, gm, sm, gub, gdb)

    @pl.when(place[2] == 0)
    def _():
        finish((own, far), held[:2], vectors, small, held[2:], copies)

    @pl.when(place[2] != 0)
    def _():
        finish((far, own), held[:2], vectors, small, held[2:], copies)


SMEM = pl.BlockSpec(memory_space=pltpu.SMEM)
VMEM = pl.BlockSpec(memory_space=pltpu.VMEM)
ANY = pl.BlockSpec(memory_space=pl.ANY)


def step_spec(shape, axis=0, held=False):
    def index(i, place):
        at = i + place[0] // PAIR if held else i
        return tuple(at if d == axis else 0 for d in range(len(shape)))

    return pl.BlockSpec(shape, index)


def constant(shape):
    return pl.BlockSpec(shape, lambda i, place: (0,) * len(shape))


def step_arrays(table, steps):
    return {
        name: (
            step_spec(shape, axis),
            jax.ShapeDtypeStruct(
                tuple(n * steps if d == axis else n for d, n in enumerate(shape)), kind
            ),
        )
        for name, (shape, kind, axis) in table.items()
    }


def call(kernel, steps, place, own, far, inputs, outputs, scratch, cost):
    own, far = list(own), list(far)
    count, other = len(own), len(far)
    scratch = dict(scratch, bits=((16, 1024), bf16, 0))
    names = list(inputs) + list(outputs) + list(scratch)

    def run(place, *refs):
        rest = refs[count + other :]
        named = SimpleNamespace(**dict(zip(names, rest)))
        named.own, named.far, named.sem = refs[:count], refs[count : count + other], rest[-1]
        kernel(place, named)

    results = pl.pallas_call(
        run,
        grid_spec=pltpu.PrefetchScalarGridSpec(
            num_scalar_prefetch=1,
            grid=(steps,),
            in_specs=[ANY] * (count + other) + [spec for spec, _ in inputs.values()],
            out_specs=[spec for spec, _ in outputs.values()],
            scratch_shapes=[pltpu.VMEM(shape, kind) for shape, kind, _ in scratch.values()]
            + [pltpu.SemaphoreType.DMA((16,))],
        ),
        out_shape=[shape for _, shape in outputs.values()],
        compiler_params=pltpu.CompilerParams(
            vmem_limit_bytes=VMEM_LIMIT, dimension_semantics=("arbitrary",)
        ),
        cost_estimate=pl.CostEstimate(flops=cost, bytes_accessed=3000000, transcendentals=0),
    )(place, *own, *far, *(operand for _, operand in inputs.values()))
    return dict(zip(outputs, results))


def body(
    tokens,
    cotangent,
    frame_ids,
    attend_gain,
    attend_shift,
    inward_weight,
    inward_bias,
    outward_weight,
    outward_bias,
    mixing_gain,
    mixing_shift,
    up_weight,
    up_bias,
    down_weight,
    down_bias,
):
    section = lax.axis_index("section")
    batch = lax.axis_index("batch")
    batches = lax.axis_size("batch")
    sequences, length, width = tokens.shape
    half = sequences // 2
    steps = half // PAIR
    place = jnp.stack([section * half, section, batch % 2]).astype(jnp.int32)

    def mine(value):
        return lax.dynamic_slice_in_dim(value, section * half, half, 0)

    def across(value):
        return lax.ppermute(value, "section", ((0, 1), (1, 0)))

    def between_cores(value):
        return lax.ppermute(value, "batch", [(b, b ^ 1) for b in range(batches)])

    everyone = ("section", "batch")
    beyond = [1 << bit for bit in range(3, batches.bit_length() - 1)]
    cubes = [
        [s * batches + base + c + 2 * i for s in range(2) for i in range(4)]
        for base in range(0, batches, 8)
        for c in range(2)
    ]

    def exchange(value):
        return lax.all_to_all(value, everyone, 0, 0, tiled=True, axis_index_groups=cubes)

    def partner(value, flip):
        return lax.ppermute(value, "batch", [(b, b ^ flip) for b in range(batches)])

    vectors, half_weights = pl.pallas_call(
        pack_kernel,
        in_specs=[VMEM] * 10,
        out_specs=[VMEM] * 2,
        out_shape=[
            jax.ShapeDtypeStruct((1, 3072), f32),
            jax.ShapeDtypeStruct((144, 1024), bf16),
        ],
    )(
        attend_gain,
        attend_shift,
        inward_bias,
        outward_bias,
        mixing_gain,
        mixing_shift,
        up_bias,
        down_bias,
        inward_weight,
        outward_weight,
    )
    own_attend = (vectors, inward_weight[0], outward_weight[0])
    half_feed = pl.pallas_call(
        pack_feed_kernel,
        in_specs=[VMEM] * 2,
        out_specs=VMEM,
        out_shape=jax.ShapeDtypeStruct((256, 1024), bf16),
    )(up_weight, down_weight)
    arrived, half_feed, held_tokens, held_cotangent = lax.optimization_barrier(
        (across(half_weights), half_feed, mine(tokens), mine(cotangent))
    )
    far_attend = (arrived, between_cores(arrived))
    arrived_feed = across(half_feed)

    def whole_frames():
        return constant((sequences, length)), frame_ids

    table = dict(ATTEND_SAVED)
    table.update(middle=BETWEEN["middle"])
    scratch = dict(ATTEND_SCRATCH)
    scratch.update(ATTEND_WEIGHTS)
    scratch.update(second=BETWEEN["second"])
    kept = call(
        attend_kernel,
        steps,
        place,
        own_attend,
        far_attend,
        dict(tokens=(step_spec((PAIR, length, 256)), held_tokens), frames=whole_frames()),
        step_arrays(table, steps),
        scratch,
        18000000000,
    )

    own = [*own_attend, up_weight[0], down_weight[0]]
    arrived_feed, kept["n2"] = lax.optimization_barrier((arrived_feed, kept["n2"]))
    far = [*far_attend, arrived_feed, between_cores(arrived_feed)]

    scratch = {}
    for table in (ATTEND_SCRATCH, BACK_SCRATCH, ATTEND_SAVED, BETWEEN, GELU_SAVED, WEIGHTS, ACC):
        scratch.update(table)
    for name in FEED_WEIGHTS:
        scratch["low_" + name] = WEIGHTS[name]
    scratch.update(e=((BOTH, 256), bf16, 0), low_second=((BOTH, 256), bf16, 0))
    outputs = {"low_" + name: pair for name, pair in step_arrays(GELU_SAVED, steps).items()}
    outputs.update(step_arrays(dict(e0=((BOTH, 256), bf16, 0)), steps))
    outputs.update(
        mine=(
            step_spec((PAIR, length, 128), 0, True),
            jax.ShapeDtypeStruct((sequences, length, 128), bf16),
        ),
        other=(
            step_spec((PAIR, length, 128)),
            jax.ShapeDtypeStruct((half, length, 128), bf16),
        ),
        keep=(constant((WIRE, 128)), jax.ShapeDtypeStruct((WIRE, 128), bf16)),
        send=(constant((WIRE, 128)), jax.ShapeDtypeStruct((WIRE, 128), bf16)),
    )
    results = call(
        middle_kernel,
        steps,
        place,
        own,
        far,
        dict(
            low_n2=(step_spec((BOTH, 256)), kept["n2"]),
            low_middle=(step_spec((BOTH, 256)), kept["middle"]),
            cotangent=(step_spec((PAIR, length, 256)), held_cotangent),
            frames=whole_frames(),
        ),
        outputs,
        scratch,
        72000000000,
    )
    kept.update(act=results["low_act"], dg=results["low_dg"])
    out_own = results["mine"]

    chunk = WIRE // 8

    def sum_cores(keep, send):
        total = keep.astype(f32) + between_cores(send).astype(f32)
        return total.astype(bf16).reshape(8, chunk, 128)

    def chunk_of(parts):
        total = jnp.sum(parts.astype(f32), axis=0).astype(bf16)
        for flip in beyond:
            total = lax.optimization_barrier(total)
            total = (total.astype(f32) + partner(total, flip).astype(f32)).astype(bf16)
        return total

    upper_parts, e0 = lax.optimization_barrier(
        (sum_cores(results["keep"], results["send"]), results["e0"])
    )
    upper_parts = exchange(upper_parts)
    out_arrived = across(results["other"])

    table = dict(ATTEND_SAVED)
    table.update(GELU_SAVED)
    inputs = {
        name: (spec, kept[name]) for name, (spec, _) in step_arrays(table, steps).items()
    }
    inputs.update(e0=(step_spec((BOTH, 256)), e0))
    for name in DEFERRED:
        inputs["whole_" + name] = (ANY, inputs.pop(name)[1])
    scratch = dict(BACK_SCRATCH)
    scratch.update(WEIGHTS)
    scratch.update(ACC)
    scratch.update(
        {name: ((2,) + ATTEND_SAVED[name][0], bf16, 0) for name in DEFERRED}
    )
    scratch.update(other=((PAIR, length, 128), bf16, 0))
    results = call(
        back_kernel,
        steps,
        place,
        own,
        far,
        inputs,
        dict(
            mine=(
                step_spec((PAIR, length, 128), 0, True),
                jax.ShapeDtypeStruct((sequences, length, 128), f32),
            ),
            early=(
                pl.BlockSpec((PAIR, length, 128), lambda i, p: (jnp.minimum(i, steps - 2), 0, 0)),
                jax.ShapeDtypeStruct((half - PAIR, length, 128), bf16),
            ),
            late=(
                constant((PAIR, length, 128)),
                jax.ShapeDtypeStruct((PAIR, length, 128), bf16),
            ),
            keep=(constant((WIRE, 128)), jax.ShapeDtypeStruct((WIRE, 128), bf16)),
            send=(constant((WIRE, 128)), jax.ShapeDtypeStruct((WIRE, 128), bf16)),
        ),
        scratch,
        40000000000,
    )
    upper_parts, out_arrived, grad_own, grad_early, grad_late, keep, send = (
        lax.optimization_barrier(
            (
                upper_parts,
                out_arrived,
                results["mine"],
                results["early"],
                results["late"],
                results["keep"],
                results["send"],
            )
        )
    )
    late_arrived = across(grad_late)
    lower_parts, late_arrived = lax.optimization_barrier((sum_cores(keep, send), late_arrived))
    lower_parts = exchange(lower_parts)
    early_arrived = across(grad_early)
    upper_chunk = chunk_of(upper_parts)

    ours = (jnp.arange(sequences) // half == section)[None, :, None]

    def assemble(held, arrived):
        arrived = jnp.concatenate([arrived, arrived], axis=0).astype(held.dtype)
        value = jnp.where(ours, held.transpose(1, 0, 2), arrived.transpose(1, 0, 2))
        return with_layout_constraint(value, Layout((0, 1, 2)))

    layer_out = assemble(out_own, out_arrived)
    lower_chunk, layer_out, early_arrived = lax.optimization_barrier(
        (chunk_of(lower_parts), layer_out, early_arrived)
    )
    spread = (4, chunk, 128)
    own_half = exchange(
        jnp.concatenate(
            [jnp.broadcast_to(lower_chunk, spread), jnp.broadcast_to(upper_chunk, spread)]
        )
    )
    input_grad = assemble(grad_own, jnp.concatenate([early_arrived, late_arrived], axis=0))
    own_half, input_grad = lax.optimization_barrier((own_half, input_grad))
    far_half = between_cores(own_half)

    grads = (
        (1, 256),
        (1, 256),
        (1, 256, 768),
        (1, 512),
        (1, 256, 256),
        (1, 256),
        (1, 256),
        (1, 256),
        (1, 256, 1024),
        (1, 1024),
        (1, 1024, 256),
        (1, 256),
    )
    finals = pl.pallas_call(
        final_kernel,
        in_specs=[SMEM] + [VMEM] * 2 + [ANY] * 2 + [VMEM] * 4,
        out_specs=[ANY if len(shape) == 3 else VMEM for shape in grads],
        out_shape=[jax.ShapeDtypeStruct(shape, f32) for shape in grads],
        scratch_shapes=[
            pltpu.VMEM((1, 256, 768), bf16),
            pltpu.VMEM((1, 256, 1024), bf16),
            pltpu.VMEM((1, 256, 768), f32),
            pltpu.VMEM((1, 256, 256), f32),
            pltpu.VMEM((1, 256, 1024), f32),
            pltpu.VMEM((1, 1024, 256), f32),
            pltpu.SemaphoreType.DMA((6,)),
        ],
        compiler_params=pltpu.CompilerParams(vmem_limit_bytes=VMEM_LIMIT),
    )(
        place,
        own_half.reshape(WIRE, 128),
        far_half.reshape(WIRE, 128),
        inward_weight,
        up_weight,
        attend_gain,
        attend_shift,
        mixing_gain,
        mixing_shift,
    )
    return (layer_out.transpose(1, 0, 2), input_grad.transpose(1, 0, 2), *finals)


def solution(mesh):
    spread = P("section", None)
    deep = P("section", None, None)
    weights = (
        spread,
        spread,
        deep,
        spread,
        deep,
        spread,
        spread,
        spread,
        deep,
        spread,
        deep,
        spread,
    )
    rows = P("batch", None, None)
    return jax.shard_map(
        body,
        mesh=mesh,
        in_specs=(rows, rows, P("batch", None)) + weights,
        out_specs=(P("batch", None, "section"),) * 2 + weights,
        check_vma=False,
    )
```

```python
import functools
from types import SimpleNamespace

import jax
import jax.numpy as jnp
from jax import lax
from jax.experimental import pallas as pl
from jax.experimental.layout import Layout, with_layout_constraint
from jax.experimental.pallas import tpu as pltpu
from jax.sharding import PartitionSpec as P

HEADS = 4
WHOLE_FRAME = 17

epsilon = 1e-05
masked_value = -1e30
log2e = 1.4426950408889634

PAIR = 2
LIVE = 368
ROWS = 384
BOTH = PAIR * ROWS
USED = BOTH - ROWS + LIVE
ONES = 16
STEP = 48
CHUNKS = tuple((at, min(STEP, LIVE - at)) for at in range(0, LIVE, STEP))
MEMBERS = tuple(range(PAIR))
TILES = ((0, 144, 0), (128, 272, 128), (256, 368, 256))
STACK = (0, 144, 416)
STACKED = 784

bf16 = jnp.bfloat16
f32 = jnp.float32


def dot(left, right):
    return jnp.dot(left, right, preferred_element_type=f32)


def dot_upper(left, right):
    return lax.dot_general(left, right, (((1,), (1,)), ((), ())), preferred_element_type=f32)


def gelu_pair(value):
    half = 0.5 + 0.5 * lax.erf(value * 0.7071067811865476)
    bell = jnp.exp2(value * value * (-0.5 * log2e) - 1.3257480647361595)
    return value * half, half + value * bell


def tree(op, parts):
    parts = list(parts)
    while len(parts) > 1:
        pairs = [op(a, b) for a, b in zip(parts[0::2], parts[1::2])]
        parts = pairs + parts[len(parts) // 2 * 2 :]
    return parts[0]


def eights(value):
    return [value[at : at + 8] for at in range(0, value.shape[0], 8)]


def twice(stat):
    return jnp.concatenate([stat, stat], axis=1)


def row_mean(value):
    mean = jnp.mean(value, axis=-1, keepdims=True)
    return jnp.broadcast_to(mean, (value.shape[0], 128))


def normalize(load, T, scales, store):
    for _, _, _, rows in chunks():
        T.mean[rows, :] = row_mean(load(rows))
    for _, _, _, rows in chunks():
        center = load(rows) - twice(T.mean[rows, :])
        T.spread[rows, :] = row_mean(center * center)
    for _, _, _, rows in chunks():
        scale = lax.rsqrt(T.spread[rows, :] + epsilon)
        scales[rows, :] = scale.astype(bf16)
        store(rows, (load(rows) - twice(T.mean[rows, :])) * twice(scale))


def norm_back(gain, g, normed, scales, T, store):
    for _, _, _, rows in chunks():
        gn = g[rows, :] * gain
        T.mean[rows, :] = row_mean(gn)
        T.slope[rows, :] = row_mean(gn * normed[rows, :].astype(f32))
    for chunk in chunks():
        rows = chunk[3]
        gn = g[rows, :] * gain - twice(T.mean[rows, :])
        back = gn - normed[rows, :].astype(f32) * twice(T.slope[rows, :])
        store(chunk, twice(scales[rows, :].astype(f32)) * back)


def masked_pair(value, head):
    lane = lax.broadcasted_iota(jnp.int32, value.shape, 1)
    keep = (lane < 64) if head % 2 == 0 else (lane >= 64)
    return jnp.where(keep, value, jnp.zeros_like(value))


def pair_lanes(head):
    return slice(128 * (head // 2), 128 * (head // 2) + 128)


def two_heads(ref, p, rows):
    value = ref[rows, 128 * p : 128 * p + 128]
    return jnp.concatenate([masked_pair(value, 0), masked_pair(value, 1)], axis=0)


def column_of(t, side):
    return slice(256 * t + 128 * side, 256 * t + 128 * side + 128)


def stack_of(t):
    return slice(STACK[t], STACK[t] + TILES[t][1])


def of(member, start, stop):
    return slice(member * ROWS + start, member * ROWS + stop)


def chunks():
    for member in MEMBERS:
        for at, size in CHUNKS:
            yield member, at, size, pl.ds(member * ROWS + at, size)


def clear_tails(*refs):
    for ref in refs:
        for member in MEMBERS:
            rows = of(member, LIVE, ROWS)
            ref[rows, :] = jnp.zeros((ROWS - LIVE,) + ref.shape[1:], ref.dtype)


def forward_attend(x, lines, W, S, T):
    vec = W.vec

    def first(rows, n):
        S.n1[rows, :] = n.astype(bf16)
        T.a[rows, :] = (n * vec[:, 0:256] + vec[:, 256:512]).astype(bf16)

    normalize(lambda rows: x[rows, :].astype(f32), T, S.r1, first)
    clear_tails(S.n1)
    a = T.a[0:USED, :]
    packed = dot(a, W.inw[...])
    T.k[0:USED, :] = packed[:, 256:512].astype(bf16)
    S.q[0:USED, :] = (packed[:, 0:256] + vec[:, 512:768]).astype(bf16)
    S.v[0:USED, :] = (packed[:, 512:768] + vec[:, 768:1024]).astype(bf16)
    clear_tails(T.k, S.q, S.v)
    for member in MEMBERS:
        frames = lines[member]
        length = frames.shape[1]
        first = jnp.sum((frames == 0).astype(f32), axis=1, keepdims=True).astype(jnp.int32)
        last = jnp.minimum(first - 1 + WHOLE_FRAME * frames, length - 1)
        T.last[:, :] = jnp.full((1, ROWS), length - 1, jnp.int32)
        T.last[:, 0:length] = last
        for t, (at, stop, sure) in enumerate(TILES):
            keys = lax.broadcasted_iota(jnp.int32, (stop - sure, 128), 0) + sure
            seen = keys <= T.last[:, at : at + 128]
            T.mask[member, t, 0 : stop - sure, :] = jnp.where(seen, 0.0, masked_value)
    power = 0.125 * log2e
    units = [(p, member) for p in range(2) for member in MEMBERS]

    def scores(u):
        p, member = units[u]
        for t, (at, stop, sure) in enumerate(TILES):
            lanes = slice(256 * t, 256 * t + 256)
            both = dot_upper(
                T.k[of(member, 0, stop), 128 * p : 128 * p + 128],
                two_heads(S.q, p, of(member, at, at + 128)),
            )
            if sure:
                T.s[u % 3, 0:sure, lanes] = both[0:sure]
            mask = twice(T.mask[member, t, 0 : stop - sure, :])
            T.s[u % 3, sure:stop, lanes] = both[sure:stop] + mask

    def strips(u, t, side):
        for start in range(0, TILES[t][1], 16):
            yield start, T.s[u % 3, start : start + 16, column_of(t, side)]

    columns = [(t, side) for t in range(3) for side in range(2)]

    def peaks(u):
        for t, side in columns:
            tops = [tree(jnp.maximum, eights(value)) for _, value in strips(u, t, side)]
            peak = jnp.max(tree(jnp.maximum, tops), axis=0, keepdims=True)
            T.peak[u % 3, :, column_of(t, side)] = peak * power

    def raises(u):
        for t, side in columns:
            lanes = column_of(t, side)
            peak = T.peak[u % 3, :, lanes]
            sums = []
            for start, value in strips(u, t, side):
                value = jnp.exp2(value * power - peak)
                T.s[u % 3, start : start + 16, lanes] = value
                sums.append(value[0:8] + value[8:16])
            total = jnp.sum(tree(jnp.add, sums), axis=0, keepdims=True)
            T.share[u % 3, :, lanes] = 1.0 / total

    def shares(u):
        p, member = units[u]
        for t, side in columns:
            lanes = column_of(t, side)
            share = T.share[u % 3, :, lanes]
            for start in range(0, TILES[t][1], 16):
                value = T.s[u % 3, start : start + 16, lanes] * share
                rows = slice(STACK[t] + start, STACK[t] + start + 16)
                S.pT[member, p, rows, 128 * side : 128 * side + 128] = value.astype(bf16)

    def mix(u):
        p, member = units[u]
        for t, (at, stop, _) in enumerate(TILES):
            both = dot(
                T.vT[128 * p : 128 * p + 128, of(member, 0, stop)],
                S.pT[member, p, stack_of(t), :],
            )
            for side in range(2):
                feats = slice(128 * p + 64 * side, 128 * p + 64 * side + 64)
                value = both[64 * side : 64 * side + 64, 128 * side : 128 * side + 128]
                S.mT[feats, of(member, at, at + 128)] = value.astype(bf16)

    scores(0)
    T.vT[...] = S.v[...].T
    peaks(0)
    scores(1)
    S.kT[...] = T.k[...].T
    raises(0)
    peaks(1)
    for u in range(len(units)):
        if u + 2 < len(units):
            scores(u + 2)
        shares(u)
        if u + 1 < len(units):
            raises(u + 1)
        if u + 2 < len(units):
            peaks(u + 2)
        mix(u)
    S.mT[256 : 256 + ONES, :] = jnp.ones((ONES, BOTH), bf16)
    mixed = S.mT[0:256, :].T
    T.f[...] = dot(mixed[0:USED], W.outw[...])
    for _, _, _, rows in chunks():
        S.middle[rows, :] = x[rows, :].astype(f32) + (T.f[rows, :] + vec[:, 1024:1280])

    def second(rows, n):
        S.n2[rows, :] = n.astype(bf16)
        S.second[rows, :] = (n * vec[:, 1280:1536] + vec[:, 1536:1792]).astype(bf16)

    normalize(lambda rows: S.middle[rows, :], T, S.r2, second)
    clear_tails(S.n2, S.second)


def forward_feed(W, S, T, out):
    vec = W.vec
    second = S.second[0:USED, :]

    T.g[...] = dot(second, W.upw[...])
    for c in range(4):
        cols = slice(256 * c, 256 * c + 256)
        for member, at, size, rows in chunks():
            bias = vec[:, 1792 + 256 * c : 2048 + 256 * c]
            act, slope = gelu_pair(T.g[rows, cols] + bias)
            S.act[rows, cols] = act.astype(bf16)
            S.dg[rows, cols] = slope.astype(bf16)
    clear_tails(S.act, S.dg)
    T.g[:, 0:256] = dot(S.act[0:USED, :], W.dnw[...])
    for member, at, size, rows in chunks():
        out(member, at, size, S.middle[rows, :] + (T.g[rows, 0:256] + vec[:, 2816:3072]))


def backward_feed(e_ref, W, S, T, acc):
    vec = W.vec
    e = e_ref[0:USED, :]
    eT = e_ref[...].T
    T.n2T[0:256, :] = S.n2[...].T

    T.g[...] = dot_upper(e, W.dnw[...])
    downs = dot(eT, S.act[...])
    for c in range(4):
        cols = slice(256 * c, 256 * c + 256)
        acc[4 + c, 0:256, :] += downs[:, cols]
        for member, at, size, rows in chunks():
            slope = S.dg[rows, cols].astype(f32)
            T.gr[rows, cols] = (T.g[rows, cols] * slope).astype(bf16)
    T.g[:, 0:256] = dot_upper(T.gr[0:USED, :], W.upw[...])
    ups = dot(T.n2T[...], T.gr[...])
    for c in range(4):
        acc[c] += ups[:, 256 * c : 256 * c + 256]
    columns = []

    def middle(chunk, back):
        rows = chunk[3]
        incoming = e_ref[rows, :].astype(f32)
        columns.append(tree(jnp.add, eights(incoming)))
        middle = incoming + back
        T.gmiddle[rows, :] = middle
        T.gp[rows, :] = middle.astype(bf16)

    norm_back(vec[:, 1280:1536], T.g.at[:, 0:256], S.n2, S.r2, T, middle)
    acc[4, 256 : 256 + ONES, :] += jnp.sum(tree(jnp.add, columns), axis=0, keepdims=True)


def backward_attend(W, S, T, acc, out):
    vec = W.vec
    gp = T.gp[...]
    T.gm[0:USED, :] = dot_upper(gp[0:USED], W.outw[...]).astype(bf16)
    T.n1T[0:256, :] = S.n1[...].T
    gmT = dot_upper(W.outw[...], gp)
    for h in range(HEADS):
        feats = slice(64 * h, 64 * h + 64)
        product = gmT[feats] * S.mT[feats, :].astype(f32)
        T.inner[h : h + 1, :] = jnp.sum(product, axis=0, keepdims=True)
    units = [(p, member) for p in range(2) for member in MEMBERS]

    def slopes(u):
        p, member = units[u]
        for t, (at, stop, _) in enumerate(TILES):
            queries = of(member, at, at + 128)
            gprobs = dot_upper(
                S.v[of(member, 0, stop), 128 * p : 128 * p + 128], two_heads(T.gm, p, queries)
            )
            probs = S.pT[member, p, stack_of(t), :].astype(f32)
            inner = [T.inner[2 * p + side : 2 * p + side + 1, queries] for side in range(2)]
            slope = probs * (gprobs - jnp.concatenate(inner, axis=1))
            T.ds[u % 2, stack_of(t), :] = slope.astype(bf16)

    def gather(parts, scale=None):
        start = 0
        for t, (_, stop, _) in enumerate(TILES):
            value = tree(jnp.add, [part[start:stop] for part in parts[t:]])
            value = value if scale is None else value * scale
            yield start, stop, value.astype(bf16)
            start = stop

    def products(u):
        p, member = units[u]
        gk, gv = [], []
        for t, (at, stop, _) in enumerate(TILES):
            queries = of(member, at, at + 128)
            ds = T.ds[u % 2, stack_of(t), :]
            gk.append(dot(ds, two_heads(S.q, p, queries)))
            gv.append(dot(S.pT[member, p, stack_of(t), :], two_heads(T.gm, p, queries)))
            both = dot(S.kT[128 * p : 128 * p + 128, of(member, 0, stop)], ds) * 0.125
            for side in range(2):
                feats = slice(128 * p + 64 * side, 128 * p + 64 * side + 64)
                value = both[64 * side : 64 * side + 64, 128 * side : 128 * side + 128]
                T.gqT[feats, queries] = value.astype(bf16)
        for start, stop, value in gather(gk, 0.125):
            T.gqkv[of(member, start, stop), 256 + 128 * p : 384 + 128 * p] = value
        for start, stop, value in gather(gv):
            T.gqkv[of(member, start, stop), 512 + 128 * p : 640 + 128 * p] = value

    slopes(0)
    acc[3] += dot(S.mT[...], gp)
    for u in range(len(units)):
        if u + 1 < len(units):
            slopes(u + 1)
        products(u)
    T.gqkv[:, 0:256] = T.gqT[...].T
    T.g[:, 0:256] = dot_upper(T.gqkv[0:USED, :], W.inw[...])
    ins = dot(T.n1T[...], T.gqkv[...])
    for b in range(3):
        acc[b] += ins[:, 256 * b : 256 * b + 256]

    def finish(chunk, back):
        member, at, size, rows = chunk
        out(member, at, size, T.gmiddle[rows, :] + back)

    norm_back(vec[:, 0:256], T.g.at[:, 0:256], S.n1, S.r1, T, finish)


ATTEND_SAVED = dict(
    n1=((BOTH, 256), bf16, 0),
    r1=((BOTH, 128), bf16, 0),
    v=((BOTH, 256), bf16, 0),
    kT=((256, BOTH), bf16, 1),
    q=((BOTH, 256), bf16, 0),
    pT=((PAIR, 2, STACKED, 256), bf16, 0),
    mT=((256 + ONES, BOTH), bf16, 1),
    n2=((BOTH, 256), bf16, 0),
    r2=((BOTH, 128), bf16, 0),
)
BETWEEN = dict(second=((BOTH, 256), bf16, 0), middle=((BOTH, 256), f32, 0))
GELU_SAVED = dict(act=((BOTH, 1024), bf16, 0), dg=((BOTH, 1024), bf16, 0))
ATTEND_SCRATCH = dict(
    a=((BOTH, 256), bf16, 0),
    k=((BOTH, 256), bf16, 0),
    vT=((256, BOTH), bf16, 1),
    last=((1, ROWS), jnp.int32, 0),
    mask=((PAIR, 3, 144, 128), f32, 0),
    s=((3, LIVE, 2 * ROWS), f32, 0),
    peak=((3, 1, 2 * ROWS), f32, 0),
    share=((3, 1, 2 * ROWS), f32, 0),
    mean=((BOTH, 128), f32, 0),
    spread=((BOTH, 128), f32, 0),
    f=((USED, 256), f32, 0),
    x=((BOTH, 256), bf16, 0),
)
BACK_SCRATCH = dict(
    mean=((BOTH, 128), f32, 0),
    slope=((BOTH, 128), f32, 0),
    g=((USED, 1024), f32, 0),
    gr=((BOTH, 1024), bf16, 0),
    gp=((BOTH, 256), bf16, 0),
    gmiddle=((BOTH, 256), f32, 0),
    n1T=((256 + ONES, BOTH), bf16, 1),
    n2T=((256 + ONES, BOTH), bf16, 1),
    gm=((BOTH, 256), bf16, 0),
    inner=((8, BOTH), f32, 0),
    ds=((2, STACKED, 256), bf16, 0),
    gqT=((256, BOTH), bf16, 0),
    gqkv=((BOTH, 768), bf16, 0),
)
ATTEND_WEIGHTS = dict(
    vec=((1, 3072), f32, 0),
    inw=((256, 768), bf16, 0),
    outw=((256, 256), bf16, 0),
)
WEIGHTS = dict(
    upw=((256, 1024), bf16, 0),
    dnw=((1024, 256), bf16, 0),
)
FEED_WEIGHTS = dict(WEIGHTS, vec=ATTEND_WEIGHTS["vec"])
WEIGHTS = dict(ATTEND_WEIGHTS, **WEIGHTS)
ACC = dict(
    feed=((8, 256 + ONES, 256), f32, 0),
    attend=((4, 256 + ONES, 256), f32, 0),
)
FEED_HALF = 8 * 256 + 128
ATTEND_HALF = 4 * 256 + 128
WIRE = FEED_HALF + ATTEND_HALF
VMEM_LIMIT = 62 * 1024 * 1024


def load_padded(ref, member, source, length):
    whole = length // 16 * 16
    ref[of(member, whole, ROWS), :] = jnp.zeros((ROWS - whole, 256), bf16)
    ref[of(member, 0, length), :] = source[...]


def fetch_weights(refs, layer, place, attend, feed=None, meanwhile=None):
    vec, inw, outw = attend
    core = place[2]

    def run(pairs):
        copies = [
            pltpu.make_async_copy(source, target, refs.sem.at[i])
            for i, (source, target) in enumerate(pairs)
        ]
        for copy in copies:
            copy.start()
        if meanwhile is not None:
            meanwhile()
        for copy in copies:
            copy.wait()

    @pl.when(place[1] == layer)
    def _():
        pairs = [(refs.own[0], vec)]
        if inw is not None:
            pairs += [(refs.own[1], inw), (refs.own[2], outw)]
        if feed is not None:
            pairs += list(zip(refs.own[3:], feed))
        run(pairs)

    @pl.when(place[1] != layer)
    def _():
        pairs = [(refs.far[0].at[128:144, :], refs.bits)]
        if inw is not None:
            for i in range(2):
                at = (core if i == 0 else 1 - core) * 128
                rows = pl.ds(pl.multiple_of(at, 128), 128)
                pairs.append((refs.far[i].at[0:128, 0:768], inw.at[rows, :]))
                pairs.append((refs.far[i].at[0:128, 768:1024], outw.at[rows, :]))
        if feed is not None:
            upw, dnw = feed
            for i in range(2):
                part = refs.far[2 + i]
                at = core if i == 0 else 1 - core
                rows = pl.ds(pl.multiple_of(at * 128, 128), 128)
                pairs.append((part.at[0:128, :], upw.at[rows, :]))
                for j in range(4):
                    rows = pl.ds(pl.multiple_of(at * 512 + 128 * j, 128), 128)
                    lanes = slice(256 * j, 256 * j + 256)
                    pairs.append((part.at[128:256, lanes], dnw.at[rows, :]))
        run(pairs)
        parts = refs.bits[...].astype(f32)
        for j in range(3):
            value = parts[j : j + 1] + parts[3 + j : 4 + j] + parts[6 + j : 7 + j]
            vec[:, 1024 * j : 1024 * j + 1024] = value


def emit_rows(target, at, blocks):
    tail = at + 512 * len(blocks)
    target[tail : tail + 128, :] = jnp.zeros((128, 128), target.dtype)
    for j, block in enumerate(blocks):
        for side in range(2):
            lanes = slice(128 * side, 128 * side + 128)
            part = 2 * j + side
            target[at + 256 * part : at + 256 * part + 256, :] = block[0:256, lanes].astype(
                target.dtype
            )
            target[tail + ONES * part : tail + ONES * part + ONES, :] = block[
                256 : 256 + ONES, lanes
            ].astype(target.dtype)


def emit_half(target, at, half, acc):
    emit_rows(target, at, [acc.feed.at[4 * half + b] for b in range(4)])
    emit_rows(target, at + FEED_HALF, [acc.attend.at[2 * half + b] for b in range(2)])


def emit_halves(refs, core):
    for half in range(2):

        @pl.when(core == half)
        def _(half=half):
            emit_half(refs.keep, 0, half, refs)
            emit_half(refs.send, 0, 1 - half, refs)


def pack_kernel(*refs):
    vec, half = refs[-2:]
    inw, outw = refs[8:10]
    at = 0
    for ref in refs[:8]:
        vec[:, at : at + ref.shape[1]] = ref[...]
        at += ref.shape[1]
    rows = pl.ds(pl.multiple_of(lax.axis_index("batch") % 2 * 128, 128), 128)
    half[0:128, 0:768] = inw[0, rows, :]
    half[0:128, 768:1024] = outw[0, rows, :]
    rest = jnp.concatenate([vec[:, 1024 * j : 1024 * j + 1024] for j in range(3)], axis=0)
    parts = []
    for _ in range(3):
        part = rest.astype(bf16).astype(f32)
        parts.append(part)
        rest = rest - part
    parts.append(jnp.zeros((7, 1024), f32))
    half[128:144, :] = jnp.concatenate(parts, axis=0).astype(bf16)


def pack_feed_kernel(upw, dnw, half):
    core = lax.axis_index("batch") % 2
    half[0:128, :] = upw[0, pl.ds(pl.multiple_of(core * 128, 128), 128), :]
    for j in range(4):
        rows = pl.ds(pl.multiple_of(core * 512 + 128 * j, 128), 128)
        half[128:256, 256 * j : 256 * j + 256] = dnw[0, rows, :]


def zero(refs):
    for ref in refs:
        ref[...] = jnp.zeros(ref.shape, ref.dtype)


def set_ones(*refs):
    for ref in refs:
        ref[256 : 256 + ONES, :] = jnp.ones((ONES, BOTH), bf16)


def attend_kernel(place, refs):
    step = pl.program_id(0)

    @pl.when(step == 0)
    def _():
        fetch_weights(refs, 0, place, (refs.vec, refs.inw, refs.outw))

    length = refs.frames.shape[1]
    lines = []
    for member in MEMBERS:
        load_padded(refs.x, member, refs.tokens.at[member], length)
        lines.append(refs.frames[pl.ds(place[0] + PAIR * step + member, 1), :])
    forward_attend(refs.x, lines, refs, refs, refs)
    for _, _, _, rows in chunks():
        refs.slim[rows, :] = refs.middle[rows, :].astype(bf16)


def middle_kernel(place, refs):
    step = pl.program_id(0)

    @pl.when(step == 0)
    def _():
        def clear():
            zero([refs.feed, refs.attend])
            clear_tails(refs.gqkv, refs.gr, refs.gp, refs.gm, refs.x, refs.low_second)
            set_ones(refs.n1T, refs.n2T)

        held = (refs.low_vec, None, None)
        fetch_weights(refs, 0, place, held, (refs.low_upw, refs.low_dnw), clear)
        held = (refs.vec, refs.inw, refs.outw)
        fetch_weights(refs, 1, place, held, (refs.upw, refs.dnw))

    length = refs.frames.shape[1]
    upper = place[1] > 0
    lower = SimpleNamespace(upw=refs.low_upw, dnw=refs.low_dnw, vec=refs.low_vec)
    below = SimpleNamespace(
        second=refs.low_second, middle=refs.low_middle, act=refs.low_act, dg=refs.low_dg
    )

    def out_lower(member, at, size, rows):
        refs.x[of(member, at, at + size), :] = rows.astype(bf16)

    def out(member, at, size, rows):
        size = min(size, length - at)
        rows = rows[:size].astype(bf16)
        low, high = rows[:, 0:128], rows[:, 128:256]
        refs.mine[member, at : at + size, :] = jnp.where(upper, high, low)
        refs.other[member, at : at + size, :] = jnp.where(upper, low, high)

    def out_back(member, at, size, rows):
        refs.e0[of(member, at, at + size), :] = rows.astype(bf16)

    lines = []
    for member in MEMBERS:
        load_padded(refs.e, member, refs.cotangent.at[member], length)
        lines.append(refs.frames[pl.ds(place[0] + PAIR * step + member, 1), :])
    for member, at, size, rows in chunks():
        n = refs.low_n2[rows, :].astype(f32)
        second = n * refs.low_vec[:, 1280:1536] + refs.low_vec[:, 1536:1792]
        refs.low_second[rows, :] = second.astype(bf16)
    forward_feed(lower, below, refs, out_lower)
    forward_attend(refs.x, lines, refs, refs, refs)
    forward_feed(refs, refs, refs, out)
    backward_feed(refs.e, refs, refs, refs, refs.feed)
    clear_tails(refs.e0)
    backward_attend(refs, refs, refs, refs.attend, out_back)

    @pl.when(step == pl.num_programs(0) - 1)
    def _():
        emit_halves(refs, place[2])


DEFERRED = ("v", "kT", "q", "pT", "mT", "n1", "r1")


def back_kernel(place, refs):
    step = pl.program_id(0)

    @pl.when(step == 0)
    def _():
        def clear():
            zero([refs.feed, refs.attend])
            clear_tails(refs.gqkv, refs.gr, refs.gp, refs.gm)
            set_ones(refs.n1T, refs.n2T)

        held = (refs.vec, refs.inw, refs.outw)
        fetch_weights(refs, 0, place, held, (refs.upw, refs.dnw), clear)

    length = refs.mine.shape[1]
    upper = place[1] > 0

    def out(member, at, size, rows):
        size = min(size, length - at)
        low, high = rows[:size, 0:128], rows[:size, 128:256]
        refs.mine[member, at : at + size, :] = jnp.where(upper, high, low)
        refs.other[member, at : at + size, :] = jnp.where(upper, low, high).astype(bf16)

    def fetches(at_step):
        slot = at_step % 2
        for i, name in enumerate(DEFERRED):
            shape, _, axis = ATTEND_SAVED[name]
            at = at_step * shape[axis]
            if shape[axis] > PAIR:
                at = pl.multiple_of(at, 128)
            where = [slice(None)] * len(shape)
            where[axis] = pl.ds(at, shape[axis])
            source = getattr(refs, "whole_" + name).at[tuple(where)]
            target = getattr(refs, name).at[slot]
            yield pltpu.make_async_copy(source, target, refs.sem.at[7 * slot + i])

    @pl.when(step == 0)
    def _():
        for copy in fetches(step):
            copy.start()

    backward_feed(refs.e0, refs, refs, refs, refs.feed)
    for copy in fetches(step):
        copy.wait()

    @pl.when(step < pl.num_programs(0) - 1)
    def _():
        for copy in fetches(step + 1):
            copy.start()

    held = {name: getattr(refs, name).at[step % 2] for name in DEFERRED}
    backward_attend(refs, SimpleNamespace(**held), refs, refs.attend, out)
    last = step == pl.num_programs(0) - 1

    @pl.when(jnp.logical_not(last))
    def _():
        refs.early[...] = refs.other[...]

    @pl.when(last)
    def _():
        refs.late[...] = refs.other[...]

    @pl.when(step == pl.num_programs(0) - 1)
    def _():
        emit_halves(refs, place[2])


def column(row):
    return jnp.broadcast_to(row, (8, 256)).T[:, 0:1]


def line(value):
    return jnp.broadcast_to(value, (256, 128)).T[0:1]


def finish(halves, inw, upw, again, ashift, mgain, mshift, outs):
    ga, sa, giw, gib, gow, gob, gm, sm, guw, gub, gdw, gdb = outs

    def block(half, at, count, part):
        start, tail = at + 256 * part, at + 512 * count + ONES * part
        rows = halves[half][start : start + 256, :].astype(f32)
        return rows, halves[half][tail : tail + ONES, :].astype(f32)[0:1]

    gain, shift = column(mgain[...]), column(mshift[...])
    of_gain, of_shift = [], []
    for part in range(8):
        rows, sums = block(0, 0, 4, part)
        lanes = slice(128 * part, 128 * part + 128)
        guw[0, :, lanes] = gain * rows + shift * sums
        gub[:, lanes] = sums
        weight = upw[0, :, lanes].astype(f32)
        of_gain.append(weight * rows)
        of_shift.append(weight * sums)
    gm[...] = line(jnp.sum(tree(jnp.add, of_gain), axis=1, keepdims=True))
    sm[...] = line(jnp.sum(tree(jnp.add, of_shift), axis=1, keepdims=True))
    for part in range(8):
        rows, sums = block(1, 0, 4, part)
        gdw[0, 128 * part : 128 * part + 128, :] = rows.T
        if part < 2:
            gdb[:, 128 * part : 128 * part + 128] = sums
    gain, shift = column(again[...]), column(ashift[...])
    of_gain, of_shift = [], []
    for part in range(8):
        rows, sums = block(part // 4, FEED_HALF, 2, part % 4)
        if part < 6:
            lanes = slice(128 * part, 128 * part + 128)
            giw[0, :, lanes] = gain * rows + shift * sums
            weight = inw[0, :, lanes].astype(f32)
            of_gain.append(weight * rows)
            of_shift.append(weight * sums)
            if part < 2:
                gib[:, lanes] = sums
            elif part >= 4:
                gib[:, 128 * part - 256 : 128 * part - 128] = sums
        else:
            lanes = slice(128 * (part - 6), 128 * (part - 6) + 128)
            gow[0, :, lanes] = rows
            gob[:, lanes] = sums
    ga[...] = line(jnp.sum(tree(jnp.add, of_gain), axis=1, keepdims=True))
    sa[...] = line(jnp.sum(tree(jnp.add, of_shift), axis=1, keepdims=True))


def final_kernel(place, own, far, *refs):
    weights, outs = refs[:6], refs[6:]

    @pl.when(place[2] == 0)
    def _():
        finish((own, far), *weights, outs)

    @pl.when(place[2] != 0)
    def _():
        finish((far, own), *weights, outs)


SMEM = pl.BlockSpec(memory_space=pltpu.SMEM)
VMEM = pl.BlockSpec(memory_space=pltpu.VMEM)
ANY = pl.BlockSpec(memory_space=pl.ANY)


def step_spec(shape, axis=0, held=False):
    def index(i, place):
        at = i + place[0] // PAIR if held else i
        return tuple(at if d == axis else 0 for d in range(len(shape)))

    return pl.BlockSpec(shape, index)


def constant(shape):
    return pl.BlockSpec(shape, lambda i, place: (0,) * len(shape))


def step_arrays(table, steps):
    return {
        name: (
            step_spec(shape, axis),
            jax.ShapeDtypeStruct(
                tuple(n * steps if d == axis else n for d, n in enumerate(shape)), kind
            ),
        )
        for name, (shape, kind, axis) in table.items()
    }


def call(kernel, steps, place, own, far, inputs, outputs, scratch, cost):
    own, far = list(own), list(far)
    count, other = len(own), len(far)
    scratch = dict(scratch, bits=((16, 1024), bf16, 0))
    names = list(inputs) + list(outputs) + list(scratch)

    def run(place, *refs):
        rest = refs[count + other :]
        named = SimpleNamespace(**dict(zip(names, rest)))
        named.own, named.far, named.sem = refs[:count], refs[count : count + other], rest[-1]
        kernel(place, named)

    results = pl.pallas_call(
        run,
        grid_spec=pltpu.PrefetchScalarGridSpec(
            num_scalar_prefetch=1,
            grid=(steps,),
            in_specs=[ANY] * (count + other) + [spec for spec, _ in inputs.values()],
            out_specs=[spec for spec, _ in outputs.values()],
            scratch_shapes=[pltpu.VMEM(shape, kind) for shape, kind, _ in scratch.values()]
            + [pltpu.SemaphoreType.DMA((16,))],
        ),
        out_shape=[shape for _, shape in outputs.values()],
        compiler_params=pltpu.CompilerParams(
            vmem_limit_bytes=VMEM_LIMIT, dimension_semantics=("arbitrary",)
        ),
        cost_estimate=pl.CostEstimate(flops=cost, bytes_accessed=3000000, transcendentals=0),
    )(place, *own, *far, *(operand for _, operand in inputs.values()))
    return dict(zip(outputs, results))


def body(
    tokens,
    cotangent,
    frame_ids,
    attend_gain,
    attend_shift,
    inward_weight,
    inward_bias,
    outward_weight,
    outward_bias,
    mixing_gain,
    mixing_shift,
    up_weight,
    up_bias,
    down_weight,
    down_bias,
):
    section = lax.axis_index("section")
    batch = lax.axis_index("batch")
    batches = lax.axis_size("batch")
    sequences, length, width = tokens.shape
    half = sequences // 2
    steps = half // PAIR
    place = jnp.stack([section * half, section, batch % 2]).astype(jnp.int32)

    def mine(value):
        return lax.dynamic_slice_in_dim(value, section * half, half, 0)

    def across(value):
        return lax.ppermute(value, "section", ((0, 1), (1, 0)))

    def between_cores(value):
        return lax.ppermute(value, "batch", [(b, b ^ 1) for b in range(batches)])

    everyone = ("section", "batch")
    beyond = [1 << bit for bit in range(3, batches.bit_length() - 1)]
    cubes = [
        [s * batches + base + c + 2 * i for s in range(2) for i in range(4)]
        for base in range(0, batches, 8)
        for c in range(2)
    ]

    def exchange(value):
        return lax.all_to_all(value, everyone, 0, 0, tiled=True, axis_index_groups=cubes)

    def partner(value, flip):
        return lax.ppermute(value, "batch", [(b, b ^ flip) for b in range(batches)])

    vectors, half_weights = pl.pallas_call(
        pack_kernel,
        in_specs=[VMEM] * 10,
        out_specs=[VMEM] * 2,
        out_shape=[
            jax.ShapeDtypeStruct((1, 3072), f32),
            jax.ShapeDtypeStruct((144, 1024), bf16),
        ],
    )(
        attend_gain,
        attend_shift,
        inward_bias,
        outward_bias,
        mixing_gain,
        mixing_shift,
        up_bias,
        down_bias,
        inward_weight,
        outward_weight,
    )
    own_attend = (vectors, inward_weight[0], outward_weight[0])
    half_feed = pl.pallas_call(
        pack_feed_kernel,
        in_specs=[VMEM] * 2,
        out_specs=VMEM,
        out_shape=jax.ShapeDtypeStruct((256, 1024), bf16),
    )(up_weight, down_weight)
    arrived, half_feed, held_tokens, held_cotangent, place = lax.optimization_barrier(
        (across(half_weights), half_feed, mine(tokens), mine(cotangent), place)
    )
    far_attend = (arrived, between_cores(arrived))
    arrived_feed = across(half_feed)

    def whole_frames():
        return constant((sequences, length)), frame_ids

    table = dict(ATTEND_SAVED)
    table.update(slim=((BOTH, 256), bf16, 0))
    scratch = dict(ATTEND_SCRATCH)
    scratch.update(ATTEND_WEIGHTS)
    scratch.update(BETWEEN)
    kept = call(
        attend_kernel,
        steps,
        place,
        own_attend,
        far_attend,
        dict(tokens=(step_spec((PAIR, length, 256)), held_tokens), frames=whole_frames()),
        step_arrays(table, steps),
        scratch,
        18000000000,
    )

    own = [*own_attend, up_weight[0], down_weight[0]]
    arrived_feed, kept["n2"] = lax.optimization_barrier((arrived_feed, kept["n2"]))
    far = [*far_attend, arrived_feed, between_cores(arrived_feed)]

    scratch = {}
    for table in (ATTEND_SCRATCH, BACK_SCRATCH, ATTEND_SAVED, BETWEEN, GELU_SAVED, WEIGHTS, ACC):
        scratch.update(table)
    for name in FEED_WEIGHTS:
        scratch["low_" + name] = WEIGHTS[name]
    scratch.update(e=((BOTH, 256), bf16, 0), low_second=((BOTH, 256), bf16, 0))
    outputs = {"low_" + name: pair for name, pair in step_arrays(GELU_SAVED, steps).items()}
    outputs.update(step_arrays(dict(e0=((BOTH, 256), bf16, 0)), steps))
    outputs.update(
        mine=(
            step_spec((PAIR, length, 128), 0, True),
            jax.ShapeDtypeStruct((sequences, length, 128), bf16),
        ),
        other=(
            step_spec((PAIR, length, 128)),
            jax.ShapeDtypeStruct((half, length, 128), bf16),
        ),
        keep=(constant((WIRE, 128)), jax.ShapeDtypeStruct((WIRE, 128), bf16)),
        send=(constant((WIRE, 128)), jax.ShapeDtypeStruct((WIRE, 128), bf16)),
    )
    results = call(
        middle_kernel,
        steps,
        place,
        own,
        far,
        dict(
            low_n2=(step_spec((BOTH, 256)), kept["n2"]),
            low_middle=(step_spec((BOTH, 256)), kept["slim"]),
            cotangent=(step_spec((PAIR, length, 256)), held_cotangent),
            frames=whole_frames(),
        ),
        outputs,
        scratch,
        72000000000,
    )
    kept.update(act=results["low_act"], dg=results["low_dg"])
    out_own = results["mine"]

    chunk = WIRE // 8

    def sum_cores(keep, send):
        total = keep.astype(f32) + between_cores(send).astype(f32)
        return total.astype(bf16).reshape(8, chunk, 128)

    def chunk_of(parts):
        total = jnp.sum(parts.astype(f32), axis=0).astype(bf16)
        for flip in beyond:
            total = lax.optimization_barrier(total)
            total = (total.astype(f32) + partner(total, flip).astype(f32)).astype(bf16)
        return total

    upper_parts, e0 = lax.optimization_barrier(
        (sum_cores(results["keep"], results["send"]), results["e0"])
    )
    upper_parts = exchange(upper_parts)
    out_arrived = across(results["other"])

    table = dict(ATTEND_SAVED)
    table.update(GELU_SAVED)
    inputs = {
        name: (spec, kept[name]) for name, (spec, _) in step_arrays(table, steps).items()
    }
    inputs.update(e0=(step_spec((BOTH, 256)), e0))
    for name in DEFERRED:
        inputs["whole_" + name] = (ANY, inputs.pop(name)[1])
    scratch = dict(BACK_SCRATCH)
    scratch.update(WEIGHTS)
    scratch.update(ACC)
    scratch.update(
        {name: ((2,) + ATTEND_SAVED[name][0], bf16, 0) for name in DEFERRED}
    )
    scratch.update(other=((PAIR, length, 128), bf16, 0))
    results = call(
        back_kernel,
        steps,
        place,
        own,
        far,
        inputs,
        dict(
            mine=(
                step_spec((PAIR, length, 128), 0, True),
                jax.ShapeDtypeStruct((sequences, length, 128), f32),
            ),
            early=(
                pl.BlockSpec((PAIR, length, 128), lambda i, p: (jnp.minimum(i, steps - 2), 0, 0)),
                jax.ShapeDtypeStruct((half - PAIR, length, 128), bf16),
            ),
            late=(
                constant((PAIR, length, 128)),
                jax.ShapeDtypeStruct((PAIR, length, 128), bf16),
            ),
            keep=(constant((WIRE, 128)), jax.ShapeDtypeStruct((WIRE, 128), bf16)),
            send=(constant((WIRE, 128)), jax.ShapeDtypeStruct((WIRE, 128), bf16)),
        ),
        scratch,
        40000000000,
    )
    upper_parts, out_arrived, grad_own, grad_early, grad_late, keep, send = (
        lax.optimization_barrier(
            (
                upper_parts,
                out_arrived,
                results["mine"],
                results["early"],
                results["late"],
                results["keep"],
                results["send"],
            )
        )
    )
    late_arrived = across(grad_late)
    lower_parts, late_arrived = lax.optimization_barrier((sum_cores(keep, send), late_arrived))
    lower_parts = exchange(lower_parts)
    early_arrived = across(grad_early)
    upper_chunk = chunk_of(upper_parts)

    ours = (jnp.arange(sequences) // half == section)[None, :, None]

    def assemble(held, arrived):
        arrived = jnp.concatenate([arrived, arrived], axis=0).astype(held.dtype)
        value = jnp.where(ours, held.transpose(1, 0, 2), arrived.transpose(1, 0, 2))
        return with_layout_constraint(value, Layout((0, 1, 2)))

    layer_out = assemble(out_own, out_arrived)
    lower_chunk, layer_out, early_arrived = lax.optimization_barrier(
        (chunk_of(lower_parts), layer_out, early_arrived)
    )
    spread = (4, chunk, 128)
    own_half = exchange(
        jnp.concatenate(
            [jnp.broadcast_to(lower_chunk, spread), jnp.broadcast_to(upper_chunk, spread)]
        )
    )
    input_grad = assemble(grad_own, jnp.concatenate([early_arrived, late_arrived], axis=0))
    own_half, input_grad = lax.optimization_barrier((own_half, input_grad))
    far_half = between_cores(own_half)

    grads = (
        (1, 256),
        (1, 256),
        (1, 256, 768),
        (1, 512),
        (1, 256, 256),
        (1, 256),
        (1, 256),
        (1, 256),
        (1, 256, 1024),
        (1, 1024),
        (1, 1024, 256),
        (1, 256),
    )
    finals = pl.pallas_call(
        final_kernel,
        in_specs=[SMEM] + [VMEM] * 8,
        out_specs=[VMEM] * 12,
        out_shape=[jax.ShapeDtypeStruct(shape, f32) for shape in grads],
        compiler_params=pltpu.CompilerParams(vmem_limit_bytes=VMEM_LIMIT),
    )(
        place,
        own_half.reshape(WIRE, 128),
        far_half.reshape(WIRE, 128),
        inward_weight,
        up_weight,
        attend_gain,
        attend_shift,
        mixing_gain,
        mixing_shift,
    )
    return (layer_out.transpose(1, 0, 2), input_grad.transpose(1, 0, 2), *finals)


def solution(mesh):
    spread = P("section", None)
    deep = P("section", None, None)
    weights = (
        spread,
        spread,
        deep,
        spread,
        deep,
        spread,
        spread,
        spread,
        deep,
        spread,
        deep,
        spread,
    )
    rows = P("batch", None, None)
    return jax.shard_map(
        body,
        mesh=mesh,
        in_specs=(rows, rows, P("batch", None)) + weights,
        out_specs=(P("batch", None, "section"),) * 2 + weights,
        check_vma=False,
    )
```
